32 devices in a mesh: walk: 4 (over y, x), chol: 8 (over z, core).
Axes of the slice: x: 2, y: 2, z: 4, core: 2. Of those that a mesh axis runs over, the one named last changes fastest.
Arguments:
- trial: float32 [512, 64], replicated
- walkers: float32 [64, 512, 64], P(('walk', 'chol')), as said below
- chol: float32 [2560, 262144], P(None, ('walk', 'chol'))
- field_noise: float32 [64, 2560], P(('walk', 'chol')), may hold values from -6 to 6
- log_weight: float32 [64], P(('walk', 'chol')), may hold values from -1 to 1
- parent: int32 [64], P(('walk', 'chol')), may hold values from 0 to 63, as said below
Outputs:
- new_walkers: float32 [64, 512, 64], P(('walk', 'chol'))
- new_log_weight: float32 [64], P(('walk', 'chol'))
The draws below stay inside these ranges and needn't reach their ends.
Inputs may be any that keep to these rules, and one draw needn't show every extreme that they name: parent[w] // 16 equals w // 16: a walker copies one of the walkers whose slots share its index along walk; some parents are copied many times and others not at all. trial and walkers are such that intersection[w] has a dominant diagonal.
All inputs are finite; a program needn't handle non-finite values.
Results may differ from the reference program's by a relative error of at most 0.0003.
Values sent between devices are 32-bit elements; how exact they have to be, the bound alone decides.
No kernel may reach another device: no remote copies, remote signals or barrier semaphores. Data moves between devices by JAX's collectives and lax.ppermute only.
A program may use at most 128 MiB of HBM per device.

```python
import jax
import jax.numpy as jnp
from jax import lax

M = 512
N = 64
NCHOL = 2560
TERMS = 6
WALKERS = 64
GROUP = 16


def pivot_pattern():
    rows = jnp.arange(M)[:, None]
    columns = jnp.arange(N)[None, :]
    return (rows == columns * (M // N)).astype(jnp.float32)


def draw_trial(key, part):
    noise = jax.random.normal(key, (M, N), jnp.float32)
    return pivot_pattern() + 0.03 * noise


def draw_walkers(key, part):
    first_key = jax.random.fold_in(jax.random.fold_in(key, 11), 0)
    noise = jax.random.normal(first_key, (WALKERS, M, N), jnp.float32)
    values = pivot_pattern()[None, :, :] + 0.02 * noise
    return values


def draw_chol(key, part):
    first_key, second_key = jax.random.split(jax.random.fold_in(key, 23))
    noise = 0.014 * jax.random.normal(first_key, (NCHOL, M * M), jnp.float32)
    amplitude = 0.016 * jax.random.normal(second_key, (NCHOL, 1), jnp.float32)
    pairs = jnp.arange(M * M)[None, :]
    return noise + jnp.where(pairs % (M + 1) == 0, amplitude, 0.0)


def draw_parent(key, part):
    first_key, second_key, third_key = jax.random.split(jax.random.fold_in(key, 37), 3)
    first_draw = jax.random.randint(first_key, (WALKERS,), 0, GROUP)
    second_draw = jax.random.randint(second_key, (WALKERS,), 0, GROUP)
    offsets = jax.random.randint(third_key, (WALKERS // GROUP,), 0, GROUP)
    slots = jnp.arange(WALKERS)
    groups = slots // GROUP
    local_parent = (first_draw * second_draw // GROUP + offsets[groups]) % GROUP
    return (groups * GROUP + local_parent).astype(jnp.int32)


def shard_levels(rng, extent, shards, low, largest):
    def one(dim, blocks):
        draws = jax.random.uniform(jax.random.fold_in(jax.random.fold_in(rng, 6), dim), (blocks,), jnp.float32, low / len(shards), largest / len(shards))
        return jnp.repeat(jnp.exp(draws), extent[dim] // blocks).reshape((-1,) + (1,) * (len(extent) - dim - 1))

    loudness = one(*shards[0])
    for cut in shards[1:]:
        loudness = loudness * one(*cut)
    return loudness


def scatter_about(rng, extent, scale, most, pieces=(), kind=jnp.bfloat16):
    entries = jax.random.normal(rng, extent, jnp.float32) * scale
    if len(pieces) > 0:
        entries = shard_levels(rng, extent, pieces, -0.22, 0.18) * entries
    return jnp.clip(entries, min=-most, max=most).astype(kind)


def setup_inputs(seed: int = 0) -> dict:
    arg_keys = jax.random.split(jax.random.key(seed), 7)
    return {
        "trial": draw_trial(jax.random.fold_in(arg_keys[6], 71), 0),
        "walkers": draw_walkers(jax.random.fold_in(arg_keys[6], 71), 0),
        "chol": draw_chol(jax.random.fold_in(arg_keys[6], 71), 0),
        "field_noise": scatter_about(arg_keys[3], (WALKERS, NCHOL), 1.0, 6.0, ((0, 32),), jnp.float32),
        "log_weight": jnp.clip(jax.random.uniform(arg_keys[4], (WALKERS,), jnp.float32, -1.0, 1.0) * shard_levels(arg_keys[4], (WALKERS,), ((0, 32),), -0.4, 0.0), -1.0, 1.0),
        "parent": draw_parent(jax.random.fold_in(arg_keys[6], 71), 0),
    }


PRECISE = lax.Precision.HIGHEST
TIME_ROOT = 0.1

def solve_single(factor, intersection):
    return jax.scipy.linalg.cho_solve((factor, True), intersection.T)

def greens(trial, walkers):
    intersection = jnp.einsum('mn,wmk->wnk', trial, walkers, precision=PRECISE)
    normal = jnp.einsum('wkn,wkm->wnm', intersection, intersection, precision=PRECISE)
    factor = jnp.linalg.cholesky(normal)
    inverse = jax.vmap(solve_single)(factor, intersection)
    rotated = jnp.einsum('wmn,wnk->wmk', walkers, inverse, precision=PRECISE)
    return jnp.einsum('wmk,ik->wmi', rotated, trial, precision=PRECISE)

def taylor(potential, walkers):
    running = walkers
    taylor_term = walkers
    for order in range(1, TERMS):
        taylor_term = jnp.einsum('wij,wjn->win', potential, taylor_term, precision=PRECISE) / order
        running = running + taylor_term
    return running

def reference(trial, walkers, chol, field_noise, log_weight, parent):
    greens_matrix = greens(trial, walkers).reshape(WALKERS, M * M)
    bias = lax.dot_general(greens_matrix.astype(jnp.float32), chol.astype(jnp.float32), (((1,), (1,)), ((), ())), precision=PRECISE, preferred_element_type=jnp.float32)
    bias_shift = TIME_ROOT * bias
    fields = field_noise - bias_shift
    weight = log_weight + jnp.sum(0.5 * bias_shift * bias_shift - field_noise * bias_shift, axis=1)
    potential = TIME_ROOT * jnp.dot(fields.astype(jnp.float32), chol.astype(jnp.float32), precision=PRECISE, preferred_element_type=jnp.float32)
    propagated = taylor(potential.reshape(WALKERS, M, M), walkers)
    return (jnp.take(propagated, parent, axis=0), jnp.take(weight, parent, axis=0))
```

```python
import functools
import math

import jax
import jax.numpy as jnp
from jax import lax
from jax.experimental import pallas as pl
from jax.experimental.pallas import tpu as pltpu
from jax.sharding import PartitionSpec as P

TERMS = 6
PRECISE = lax.Precision.HIGHEST
TIME_ROOT = 0.1
BOTH = ("walk", "chol")
LANES = 128
SUBLANES = 8
F32 = jnp.float32
BF16 = jnp.bfloat16
VMEM_BYTES = 48 * 1024 * 1024


def params():
    return pltpu.CompilerParams(vmem_limit_bytes=VMEM_BYTES)


def whole(shape):
    zeros = (0,) * len(shape)
    return pl.BlockSpec(shape, lambda *_: zeros)


def dot(a, b):
    return jnp.dot(a, b, preferred_element_type=F32)


def dot_nt(a, b):
    return lax.dot_general(a, b, (((1,), (1,)), ((), ())), preferred_element_type=F32)


def split(x):
    high = x.astype(BF16)
    low = (x - high.astype(F32)).astype(BF16)
    return high, low


def rotate_kernel(devices, parent, weight, trial, walkers, noise, sent, pack):
    own, orbitals, occupied = walkers.shape
    half = orbitals // devices // 2
    rows = jax.lax.broadcasted_iota(jnp.int32, (occupied, 1), 0)
    state = []
    for s in range(own):
        crossed = lax.dot_general(
            walkers[s], trial[...], (((0,), (0,)), ((), ())),
            precision=PRECISE, preferred_element_type=F32,
        )
        normal = lax.dot_general(
            crossed, crossed, (((1,), (1,)), ((), ())),
            precision=PRECISE, preferred_element_type=F32,
        )
        state.append(jnp.concatenate([normal, crossed], axis=1))
    for k in range(occupied):
        for s in range(own):
            m = state[s]
            pivot = m[k : k + 1, :]
            scaled = pivot / m[k : k + 1, k : k + 1]
            state[s] = jnp.where(rows == k, scaled, m - m[:, k : k + 1] * scaled)
    lane = jax.lax.broadcasted_iota(jnp.int32, (SUBLANES, LANES), 1)
    extra = jnp.zeros((SUBLANES, LANES), F32)
    levels = jnp.zeros((SUBLANES, LANES), F32)
    for s in range(own):
        inverse = state[s][:, occupied:]
        rotated = jnp.dot(walkers[s], inverse, precision=PRECISE, preferred_element_type=F32)
        blocks = rotated.reshape(devices, 2, half, occupied)
        sent[:, s * half : (s + 1) * half, :] = jnp.concatenate([blocks[:, 0], blocks[:, 1]], axis=2)
        extra = jnp.where(lane == s, parent[s].astype(F32), extra)
        levels = jnp.where(lane == s, weight[s], levels)
        pack[:orbitals, s * occupied : (s + 1) * occupied] = walkers[s]
        width = noise.shape[1] // LANES
        for t in range(width):
            at = orbitals + s * width + t
            pack[at : at + 1, :] = noise[s : s + 1, t * LANES : (t + 1) * LANES]
    tail = sent.shape[1] - own * half
    sent[:, own * half :, :] = jnp.broadcast_to(extra[None, :tail], (devices, tail, LANES))
    first = pack.shape[0] - SUBLANES
    pack[first:, :] = levels


def rotate_plain(devices, parent, weight, trial, walkers, noise, sent_rows, pack_rows):
    own, orbitals, occupied = walkers.shape
    half = orbitals // devices // 2
    crossed = jnp.einsum("wmk,mn->wkn", walkers, trial, precision=PRECISE)
    normal = jnp.einsum("wkn,wln->wkl", crossed, crossed, precision=PRECISE)
    factor = jnp.linalg.cholesky(normal)
    inverse = jax.vmap(lambda f, c: jax.scipy.linalg.cho_solve((f, True), c))(factor, crossed)
    rotated = jnp.einsum("wmk,wkn->wmn", walkers, inverse, precision=PRECISE)
    sent = rotated.reshape(own, devices, 2, half, occupied).transpose(1, 0, 3, 2, 4)
    sent = sent.reshape(devices, own * half, 2 * occupied)
    extra = jnp.zeros((sent_rows - own * half, LANES), F32).at[0, :own].set(parent.astype(F32))
    sent = jnp.concatenate([sent, jnp.broadcast_to(extra[None], (devices,) + extra.shape)], axis=1)
    levels = jnp.zeros((SUBLANES, LANES), F32).at[0, :own].set(weight)
    pack = jnp.concatenate(
        [walkers.transpose(1, 0, 2).reshape(orbitals, own * occupied), noise.reshape(-1, LANES), levels], axis=0
    )
    return sent, pack


def rotate(devices, parent, weight, trial, walkers, noise):
    own, orbitals, occupied = walkers.shape
    half = orbitals // devices // 2
    sent_rows = -(-(own * half + 1) // SUBLANES) * SUBLANES
    pack_rows = orbitals + noise.size // LANES + SUBLANES
    if half % SUBLANES:
        return rotate_plain(devices, parent, weight, trial, walkers, noise, sent_rows, pack_rows)
    smem = pl.BlockSpec(memory_space=pltpu.SMEM)
    return pl.pallas_call(
        functools.partial(rotate_kernel, devices),
        out_shape=(
            jax.ShapeDtypeStruct((devices, sent_rows, LANES), F32),
            jax.ShapeDtypeStruct((pack_rows, LANES), F32),
        ),
        in_specs=[smem, smem] + [pl.BlockSpec(memory_space=pltpu.VMEM)] * 3,
        out_specs=(pl.BlockSpec(memory_space=pltpu.VMEM),) * 2,
        compiler_params=params(),
    )(parent, weight, trial, walkers, noise)


def contract_kernel(trial, chol, out):
    orbitals, occupied = trial.shape
    half = chol.shape[1] // orbitals // 2
    high, low = split(trial[...])
    pair = jnp.concatenate([high, low], axis=1)
    alone = jnp.concatenate([high, jnp.zeros_like(high)], axis=1)
    lane = jax.lax.broadcasted_iota(jnp.int32, (1, 2 * occupied), 1)

    def one(i):
        chol_high, chol_low = split(chol[:, i * orbitals : (i + 1) * orbitals])
        both = dot(chol_high, pair) + dot(chol_low, alone)
        return both + pltpu.roll(both, occupied, 1)

    for i in range(half):
        out[:, i * 2 * occupied : (i + 1) * 2 * occupied] = jnp.where(lane < occupied, one(i), one(i + half))


def contract(trial, chol):
    vectors, pairs = chol.shape
    orbitals, occupied = trial.shape
    columns = pairs // orbitals * occupied
    block = 128
    return pl.pallas_call(
        contract_kernel,
        grid=(vectors // block,),
        out_shape=jax.ShapeDtypeStruct((vectors, columns), F32),
        in_specs=[whole(trial.shape), pl.BlockSpec((block, pairs), lambda g: (g, 0))],
        out_specs=pl.BlockSpec((block, columns), lambda g: (g, 0)),
        compiler_params=params(),
        cost_estimate=pl.CostEstimate(
            flops=2 * vectors * pairs * occupied * 3, bytes_accessed=4 * vectors * (pairs + columns), transcendentals=0
        ),
    )(trial, chol)


def bias_kernel(own, half, place, rotated, contracted, noise, out, high, low):
    devices = rotated.shape[0]

    @pl.when(pl.program_id(0) == 0)
    def _():
        for i in range(half):
            for s in range(own):
                part = rotated[:, s * half + i, :]
                part_high, part_low = split(part)
                high[s * devices : (s + 1) * devices, i * LANES : (i + 1) * LANES] = part_high
                low[s * devices : (s + 1) * devices, i * LANES : (i + 1) * LANES] = part_low

    b_high, b_low = split(contracted[...])
    bias = dot_nt(high[...], b_high) + dot_nt(low[...], b_high) + dot_nt(high[...], b_low)
    rows = jax.lax.broadcasted_iota(jnp.int32, (out.shape[0], 1), 0)
    value = -TIME_ROOT * bias
    for s in range(own):
        value += jnp.where(rows == s * devices + place[0], noise[s : s + 1, :], 0.0)
    out[...] = value


def partial_fields(own, half, place, rotated, contracted, noise):
    vectors, columns = contracted.shape
    devices = rotated.shape[0]
    block = 512
    return pl.pallas_call(
        functools.partial(bias_kernel, own, half),
        grid=(vectors // block,),
        out_shape=jax.ShapeDtypeStruct((own * devices, vectors), F32),
        in_specs=[
            pl.BlockSpec(memory_space=pltpu.SMEM),
            whole(rotated.shape),
            pl.BlockSpec((block, columns), lambda g: (g, 0)),
            pl.BlockSpec((own, block), lambda g: (0, g)),
        ],
        out_specs=pl.BlockSpec((own * devices, block), lambda g: (0, g)),
        scratch_shapes=[pltpu.VMEM((own * devices, columns), BF16)] * 2,
        compiler_params=params(),
    )(place, rotated, contracted, noise)


def send(x, walk_size, chol_size, target):
    return lax.ppermute(x, BOTH, [(i, target(i)) for i in range(walk_size * chol_size)])


def sum_everywhere(x, walk_size, chol_size):
    walk = lax.axis_index("walk")
    core = lax.axis_index("chol") % 2
    half = x.shape[0] // 2
    quarter = half // walk_size
    mine = lax.dynamic_slice_in_dim(x, core * half, half, 0)
    other = lax.dynamic_slice_in_dim(x, (1 - core) * half, half, 0)
    chip = mine + send(other, walk_size, chol_size, lambda i: i ^ 1)
    total = lax.dynamic_slice_in_dim(chip, walk * quarter, quarter, 0)
    got = [
        send(
            lax.dynamic_slice_in_dim(chip, (walk ^ r) * quarter, quarter, 0),
            walk_size, chol_size, lambda i, r=r: i ^ (r * chol_size),
        )
        for r in range(1, walk_size)
    ]
    for g in got:
        total = total + g
    got = [send(total, walk_size, chol_size, lambda i, r=r: i ^ (2 * r)) for r in range(1, chol_size // 2)]
    for g in got:
        total = total + g
    blocks = [total] + [
        send(total, walk_size, chol_size, lambda i, r=r: i ^ (r * chol_size)) for r in range(1, walk_size)
    ]
    here = jnp.concatenate(blocks, axis=0)
    there = send(here, walk_size, chol_size, lambda i: i ^ 1)
    return jnp.concatenate([here, there], axis=0)


def row_of(walker, own, walk_size, chol_size):
    everyone = own * walk_size * chol_size
    walk = lax.axis_index("walk")
    core = lax.axis_index("chol") % 2
    row = (walker % own) * (walk_size * chol_size) + walker // own
    half = everyone // 2
    quarter = half // walk_size
    inside = row % half
    return ((row // half) ^ core) * half + ((inside // quarter) ^ walk) * quarter + inside % quarter


def select_kernel(rows, fields, out):
    slots = fields.shape[0]
    lane = jax.lax.broadcasted_iota(jnp.int32, (slots, slots), 1)
    pick = jnp.where(lane == rows[...], 1.0, 0.0).astype(BF16)
    value = fields[...]
    first, rest = split(value)
    second, third = split(value - first.astype(F32))
    picked = dot(pick, first) + dot(pick, second) + dot(pick, third)
    high, low = split(TIME_ROOT * picked)
    out[:slots, :] = high
    out[slots:, :] = low


def select(rows, fields):
    slots, vectors = fields.shape
    block = 512
    return pl.pallas_call(
        select_kernel,
        grid=(vectors // block,),
        out_shape=jax.ShapeDtypeStruct((2 * slots, vectors), BF16),
        in_specs=[whole((slots, 1)), pl.BlockSpec((slots, block), lambda g: (0, g))],
        out_specs=pl.BlockSpec((2 * slots, block), lambda g: (0, g)),
        compiler_params=params(),
    )(rows.reshape(slots, 1), fields)


def potential_kernel(count, fields, chol, out):
    slots = fields.shape[0] // 2
    vectors = chol.shape[0]
    step = 512
    total = None
    for k in range(0, vectors, step):
        high, low = split(chol[k : k + step, :])
        both = dot(fields[:, k : k + step], high)
        value = both[:slots] + both[slots:] + dot(fields[:slots, k : k + step], low)
        total = value if total is None else total + value
    pieces = chol.shape[1] // LANES
    for t in range(pieces):
        at = pl.ds(t * count + pl.program_id(0), slots, stride=pieces * count)
        out[at, :] = total[:, t * LANES : (t + 1) * LANES]


def potential_tiles(fields, chol, orbitals, first, count):
    vectors = chol.shape[0]
    slots = fields.shape[0] // 2
    return pl.pallas_call(
        functools.partial(potential_kernel, count),
        grid=(count,),
        out_shape=jax.ShapeDtypeStruct((slots * count * orbitals // LANES, LANES), F32),
        in_specs=[whole(fields.shape), pl.BlockSpec((vectors, orbitals), lambda i: (0, first + i))],
        out_specs=whole((slots * count * orbitals // LANES, LANES)),
        compiler_params=params(),
        cost_estimate=pl.CostEstimate(
            flops=2 * slots * vectors * orbitals * count * 3,
            bytes_accessed=4 * vectors * orbitals * count,
            transcendentals=0,
        ),
    )(fields, chol)


def taylor_kernel(own, chunks, index, *refs):
    starts = refs[:own]
    tiles = refs[own : own + chunks]
    out = refs[own + chunks]
    high, low, term = refs[own + chunks + 1 :]
    orbitals, width = term.shape
    occupied = width // own
    pieces = orbitals // LANES
    devices = tiles[0].shape[0]
    count = tiles[0].shape[1] // (own * pieces)
    lane = jax.lax.broadcasted_iota(jnp.int32, (1, width), 1) // occupied
    rows = devices * own * count
    for c in range(chunks):
        for t in range(pieces):
            value = tiles[c][...].reshape(devices * own, pieces, count, LANES)[:, t].reshape(rows, LANES)
            value_high, value_low = split(value)
            high[c * rows : (c + 1) * rows, t * LANES : (t + 1) * LANES] = value_high
            low[c * rows : (c + 1) * rows, t * LANES : (t + 1) * LANES] = value_low
    total = jnp.zeros((orbitals, width), F32)
    for s in range(own):
        source = starts[s][0]
        inside = index[own + s]
        moved = source
        for shift in range(1, own):
            rolled = pltpu.roll(source, shift * occupied, 1)
            moved = jnp.where((inside + shift) % own == s, rolled, moved)
        total = jnp.where(lane == s, moved, total)
    term[...] = total
    for order in range(1, TERMS):
        term_high, term_low = split(term[...])
        pair = jnp.concatenate([term_high, term_low], axis=1)
        both = dot(high[...], pair)
        value = both[:, :width] + both[:, width:] + dot(low[...], term_high)
        value = value.reshape(chunks, devices, own, count, width)
        picked = value[:, :, 0]
        for s in range(1, own):
            picked = jnp.where(lane == s, value[:, :, s], picked)
        picked = picked / order
        placed = jnp.stack([picked[c] for c in range(chunks)], axis=1).reshape(orbitals, width)
        term[...] = placed
        total = total + placed
    for s in range(own):
        out[s] = total[:, s * occupied : (s + 1) * occupied]


def taylor_plain(index, gathered, tiles, own, orbitals, occupied):
    pieces = orbitals // LANES
    devices = tiles[0].shape[0]
    parts = [t.reshape(devices, own, pieces, -1, LANES).transpose(1, 0, 3, 2, 4) for t in tiles]
    potential = jnp.concatenate(parts, axis=2).reshape(own, orbitals, orbitals)
    picked = gathered[index[:own], :orbitals].reshape(own, orbitals, own, occupied)
    term = jnp.take_along_axis(picked, index[own:].reshape(own, 1, 1, 1), axis=2)[:, :, 0]
    running = term
    for order in range(1, TERMS):
        term = jnp.einsum("wij,wjn->win", potential, term, precision=PRECISE) / order
        running = running + term
    return running


def taylor(index, gathered, tiles, own, orbitals, occupied):
    width = own * occupied
    chunks = len(tiles)
    pieces = orbitals // LANES
    if (tiles[0].shape[1] // (own * pieces)) % SUBLANES:
        return taylor_plain(index, gathered, tiles, own, orbitals, occupied)
    rows = sum(t.shape[0] * t.shape[1] for t in tiles) // pieces

    def at(s):
        return pl.BlockSpec((1, orbitals, width), lambda i, index: (index[s], 0, 0))

    return pl.pallas_call(
        functools.partial(taylor_kernel, own, chunks),
        grid_spec=pltpu.PrefetchScalarGridSpec(
            num_scalar_prefetch=1,
            grid=(1,),
            in_specs=[at(s) for s in range(own)] + [whole(t.shape) for t in tiles],
            out_specs=whole((own, orbitals, occupied)),
            scratch_shapes=[
                pltpu.VMEM((rows, orbitals), BF16),
                pltpu.VMEM((rows, orbitals), BF16),
                pltpu.VMEM((orbitals, width), F32),
            ],
        ),
        out_shape=jax.ShapeDtypeStruct((own, orbitals, occupied), F32),
        compiler_params=params(),
    )(index, *[gathered] * own, *tiles)


def per_device(trial, walkers, chol, field_noise, log_weight, parent):
    own, orbitals, occupied = walkers.shape
    walk_size = lax.axis_size("walk")
    chol_size = lax.axis_size("chol")
    devices = walk_size * chol_size
    vectors, pairs = chol.shape
    rows_here = pairs // orbitals
    half = rows_here // 2
    place = lax.axis_index(BOTH)

    sent, pack = rotate(devices, parent, log_weight, trial, walkers, field_noise)
    rotated = lax.all_to_all(sent, BOTH, split_axis=0, concat_axis=0, tiled=True)
    gathered = lax.all_gather(pack, "chol", axis=0, tiled=False)
    contracted = contract(trial, chol)
    mine = partial_fields(own, half, place.reshape(1), rotated, contracted, field_noise)
    fields = sum_everywhere(mine, walk_size, chol_size)

    parents = rotated[:, own * half, :own].reshape(own * devices).astype(jnp.int32)
    parent_rows = row_of(parents, own, walk_size, chol_size)
    scaled = select(parent_rows, fields)

    count = math.gcd(rows_here, SUBLANES)
    tiles = []
    for first in range(0, rows_here, count):
        chunk = potential_tiles(scaled, chol, orbitals, first, count)
        chunk = chunk.reshape(devices, own * count * orbitals // LANES, LANES)
        tiles.append(lax.all_to_all(chunk, BOTH, split_axis=0, concat_axis=0, tiled=True))

    local = parent - lax.axis_index("walk") * (own * chol_size)
    source, inside = local // own, local % own
    new_walkers = taylor(
        jnp.concatenate([source, inside]), gathered, tiles, own, orbitals, occupied
    )

    width = vectors // LANES
    notes = gathered[:, orbitals : orbitals + own * width, :].reshape(own * chol_size, vectors)
    parent_noise = jnp.take(notes, local, axis=0)
    parent_level = jnp.take(gathered[:, -SUBLANES, :own].reshape(own * chol_size), local, axis=0)
    parent_fields = jnp.take(fields, row_of(parent, own, walk_size, chol_size), axis=0)
    shift = parent_noise - parent_fields
    new_log_weight = parent_level + jnp.sum(0.5 * shift * shift - parent_noise * shift, axis=1)
    return (new_walkers, new_log_weight)


def solution(mesh):
    return jax.shard_map(
        per_device,
        mesh=mesh,
        in_specs=(
            P(),
            P(BOTH, None, None),
            P(None, BOTH),
            P(BOTH, None),
            P(BOTH),
            P(BOTH),
        ),
        out_specs=(P(BOTH, None, None), P(BOTH)),
        check_vma=False,
    )
```

```python
import functools

import jax
import jax.numpy as jnp
from jax import lax
from jax.experimental import pallas as pl
from jax.experimental.pallas import tpu as pltpu
from jax.sharding import PartitionSpec as P

TERMS = 6
PRECISE = lax.Precision.HIGHEST
TIME_ROOT = 0.1
BOTH = ("walk", "chol")
LANES = 128
SUBLANES = 8
F32 = jnp.float32
BF16 = jnp.bfloat16
MIB = 1024 * 1024
FIRST_UNITS = 1


def params(mib):
    return pltpu.CompilerParams(vmem_limit_bytes=mib * MIB)


def whole(shape):
    zeros = (0,) * len(shape)
    return pl.BlockSpec(shape, lambda *_: zeros)


def dot(a, b):
    return jnp.dot(a, b, preferred_element_type=F32)


def dot_nt(a, b):
    return lax.dot_general(a, b, (((1,), (1,)), ((), ())), preferred_element_type=F32)


def split(x):
    high = x.astype(BF16)
    low = (x - high.astype(F32)).astype(BF16)
    return high, low


def rotate_kernel(devices, parent, weight, trial, walkers, noise, sent, pack, pair):
    own, occupied, orbitals = walkers.shape
    half = orbitals // devices // 2
    rows = jax.lax.broadcasted_iota(jnp.int32, (occupied, 1), 0)
    state = []
    for s in range(own):
        crossed = lax.dot_general(
            walkers[s], trial[...], (((1,), (1,)), ((), ())), precision=PRECISE, preferred_element_type=F32
        )
        normal = lax.dot_general(
            crossed, crossed, (((1,), (1,)), ((), ())), precision=PRECISE, preferred_element_type=F32
        )
        state.append(jnp.concatenate([normal, crossed], axis=1))
    for k in range(occupied):
        for s in range(own):
            m = state[s]
            pivot = m[k : k + 1, :]
            scaled = pivot / m[k : k + 1, k : k + 1]
            state[s] = jnp.where(rows == k, scaled, m - m[:, k : k + 1] * scaled)
    lane = jax.lax.broadcasted_iota(jnp.int32, (1, LANES), 1)
    packed = jnp.concatenate([walkers[s] for s in range(own)], axis=0).T
    pack[:orbitals, :] = packed
    empty = jnp.zeros((occupied, occupied), F32)
    inverse = jnp.concatenate(
        [
            jnp.concatenate([state[s][:, occupied:] if s == c else empty for c in range(own)], axis=1)
            for s in range(own)
        ],
        axis=0,
    )
    rotated = jnp.dot(packed, inverse, precision=PRECISE, preferred_element_type=F32)
    blocks = rotated.reshape(devices, 2, half, LANES)
    first, second = blocks[:, 0], blocks[:, 1]
    sent[:, :half, :] = jnp.where(lane < occupied, first, pltpu.roll(second, occupied, 2))
    sent[:, half : 2 * half, :] = jnp.where(lane < occupied, pltpu.roll(first, occupied, 2), second)
    extra = jnp.zeros((SUBLANES, LANES), F32)
    levels = jnp.zeros((SUBLANES, LANES), F32)
    width = noise.shape[1] // LANES
    for s in range(own):
        extra = jnp.where(lane == s, parent[s].astype(F32), extra)
        levels = jnp.where(lane == s, weight[s], levels)
        for t in range(width):
            at = orbitals + s * width + t
            pack[at : at + 1, :] = noise[s : s + 1, t * LANES : (t + 1) * LANES]
    tail = sent.shape[1] - own * half
    sent[:, own * half :, :] = jnp.broadcast_to(extra[None, :tail], (devices, tail, LANES))
    pack[pack.shape[0] - SUBLANES :, :] = levels
    value = jnp.concatenate([trial[...]] * 2, axis=0).T
    high, low = split(value)
    pair[...] = jnp.where(lane < occupied, high, low)


def rotate_plain(devices, parent, weight, trial, walkers, noise, sent_rows, pack_rows):
    own, occupied, orbitals = walkers.shape
    half = orbitals // devices // 2
    crossed = jnp.einsum("wkm,nm->wkn", walkers, trial, precision=PRECISE)
    normal = jnp.einsum("wkn,wln->wkl", crossed, crossed, precision=PRECISE)
    factor = jnp.linalg.cholesky(normal)
    inverse = jax.vmap(lambda f, c: jax.scipy.linalg.cho_solve((f, True), c))(factor, crossed)
    rotated = jnp.einsum("wkm,wkn->wmn", walkers, inverse, precision=PRECISE)
    sent = rotated.reshape(own, devices, 2, half, occupied).transpose(1, 0, 3, 2, 4)
    sent = sent.reshape(devices, own * half, 2 * occupied)
    extra = jnp.zeros((sent_rows - own * half, LANES), F32).at[0, :own].set(parent.astype(F32))
    sent = jnp.concatenate([sent, jnp.broadcast_to(extra[None], (devices,) + extra.shape)], axis=1)
    levels = jnp.zeros((SUBLANES, LANES), F32).at[0, :own].set(weight)
    pack = jnp.concatenate(
        [walkers.transpose(2, 0, 1).reshape(orbitals, own * occupied), noise.reshape(-1, LANES), levels], axis=0
    )
    return sent, pack, jnp.concatenate(split(trial.T), axis=1)


def rotate(devices, parent, weight, trial, walkers, noise):
    own, occupied, orbitals = walkers.shape
    half = orbitals // devices // 2
    sent_rows = -(-(own * half + 1) // SUBLANES) * SUBLANES
    pack_rows = orbitals + noise.size // LANES + SUBLANES
    if half % SUBLANES or own != 2 or own * occupied != LANES:
        return rotate_plain(devices, parent, weight, trial, walkers, noise, sent_rows, pack_rows)
    smem = pl.BlockSpec(memory_space=pltpu.SMEM)
    return pl.pallas_call(
        functools.partial(rotate_kernel, devices),
        out_shape=(
            jax.ShapeDtypeStruct((devices, sent_rows, LANES), F32),
            jax.ShapeDtypeStruct((pack_rows, LANES), F32),
            jax.ShapeDtypeStruct((orbitals, 2 * occupied), BF16),
        ),
        in_specs=[smem, smem] + [pl.BlockSpec(memory_space=pltpu.VMEM)] * 3,
        out_specs=(pl.BlockSpec(memory_space=pltpu.VMEM),) * 3,
        compiler_params=params(16),
    )(parent, weight, trial, walkers, noise)


def contract_kernel(pair, chol, out):
    orbitals = pair.shape[0]
    occupied = pair.shape[1] // 2
    half = chol.shape[1] // orbitals // 2
    lane = jax.lax.broadcasted_iota(jnp.int32, (1, 2 * occupied), 1)
    both_parts = pair[...]
    alone = jnp.where(lane < occupied, both_parts, jnp.zeros_like(both_parts))

    def one(i):
        chol_high, chol_low = split(chol[:, i * orbitals : (i + 1) * orbitals])
        both = dot(chol_high, both_parts) + dot(chol_low, alone)
        return both + pltpu.roll(both, occupied, 1)

    for i in range(half):
        out[:, i * 2 * occupied : (i + 1) * 2 * occupied] = jnp.where(lane < occupied, one(i), one(i + half))


def contract(pair, chol):
    vectors, pairs = chol.shape
    orbitals, occupied = pair.shape[0], pair.shape[1] // 2
    columns = pairs // orbitals * occupied
    block = 256
    return pl.pallas_call(
        contract_kernel,
        grid=(vectors // block,),
        out_shape=jax.ShapeDtypeStruct((vectors, columns), F32),
        in_specs=[whole(pair.shape), pl.BlockSpec((block, pairs), lambda g: (g, 0))],
        out_specs=pl.BlockSpec((block, columns), lambda g: (g, 0)),
        compiler_params=params(32),
        cost_estimate=pl.CostEstimate(
            flops=2 * vectors * pairs * occupied * 3, bytes_accessed=4 * vectors * (pairs + columns), transcendentals=0
        ),
    )(pair, chol)


def bias_kernel(own, half, place, rotated, contracted, noise, out, high, low):
    devices = rotated.shape[0]
    for i in range(half):
        for s in range(own):
            part_high, part_low = split(rotated[:, s * half + i, :])
            high[s * devices : (s + 1) * devices, i * LANES : (i + 1) * LANES] = part_high
            low[s * devices : (s + 1) * devices, i * LANES : (i + 1) * LANES] = part_low
    rows = jax.lax.broadcasted_iota(jnp.int32, (out.shape[0], 1), 0)
    block = 512
    for g in range(0, out.shape[1], block):
        b_high, b_low = split(contracted[g : g + block, :])
        bias = dot_nt(high[...], b_high) + dot_nt(low[...], b_high) + dot_nt(high[...], b_low)
        value = -TIME_ROOT * bias
        for s in range(own):
            value += jnp.where(rows == s * devices + place[0], noise[s : s + 1, g : g + block], 0.0)
        out[:, g : g + block] = value


def partial_fields(own, half, place, rotated, contracted, noise):
    vectors, columns = contracted.shape
    devices = rotated.shape[0]
    return pl.pallas_call(
        functools.partial(bias_kernel, own, half),
        out_shape=jax.ShapeDtypeStruct((own * devices, vectors), F32),
        in_specs=[pl.BlockSpec(memory_space=pltpu.SMEM)] + [pl.BlockSpec(memory_space=pltpu.VMEM)] * 3,
        out_specs=pl.BlockSpec(memory_space=pltpu.VMEM),
        scratch_shapes=[pltpu.VMEM((own * devices, columns), BF16)] * 2,
        compiler_params=params(28),
    )(place, rotated, contracted, noise)


def send(x, walk_size, chol_size, target):
    return lax.ppermute(x, BOTH, [(i, target(i)) for i in range(walk_size * chol_size)])


def sum_everywhere(x, walk_size, chol_size):
    walk = lax.axis_index("walk")
    core = lax.axis_index("chol") % 2
    half = x.shape[0] // 2
    quarter = half // walk_size
    mine = lax.dynamic_slice_in_dim(x, core * half, half, 0)
    other = lax.dynamic_slice_in_dim(x, (1 - core) * half, half, 0)
    chip = mine + send(other, walk_size, chol_size, lambda i: i ^ 1)
    total = lax.dynamic_slice_in_dim(chip, walk * quarter, quarter, 0)
    got = [
        send(
            lax.dynamic_slice_in_dim(chip, (walk ^ r) * quarter, quarter, 0),
            walk_size, chol_size, lambda i, r=r: i ^ (r * chol_size),
        )
        for r in range(1, walk_size)
    ]
    for g in got:
        total = total + g
    got = [send(total, walk_size, chol_size, lambda i, r=r: i ^ (2 * r)) for r in range(1, chol_size // 2)]
    for g in got:
        total = total + g
    blocks = [total] + [
        send(total, walk_size, chol_size, lambda i, r=r: i ^ (r * chol_size)) for r in range(1, walk_size)
    ]
    here = jnp.concatenate(blocks, axis=0)
    there = send(here, walk_size, chol_size, lambda i: i ^ 1)
    return jnp.concatenate([here, there], axis=0)


def row_of(walker, own, walk_size, chol_size):
    everyone = own * walk_size * chol_size
    walk = lax.axis_index("walk")
    core = lax.axis_index("chol") % 2
    row = (walker % own) * (walk_size * chol_size) + walker // own
    half = everyone // 2
    quarter = half // walk_size
    inside = row % half
    return ((row // half) ^ core) * half + ((inside // quarter) ^ walk) * quarter + inside % quarter


def select_kernel(rows, fields, out):
    slots = fields.shape[0]
    lane = jax.lax.broadcasted_iota(jnp.int32, (slots, slots), 1)
    pick = jnp.where(lane == rows[...], 1.0, 0.0).astype(BF16)
    value = fields[...]
    first, rest = split(value)
    second, third = split(value - first.astype(F32))
    picked = dot(pick, first) + dot(pick, second) + dot(pick, third)
    high, low = split(TIME_ROOT * picked)
    out[:slots, :] = high
    out[slots:, :] = low


def select(rows, fields):
    slots, vectors = fields.shape
    block = 512
    return pl.pallas_call(
        select_kernel,
        grid=(vectors // block,),
        out_shape=jax.ShapeDtypeStruct((2 * slots, vectors), BF16),
        in_specs=[whole((slots, 1)), pl.BlockSpec((slots, block), lambda g: (0, g))],
        out_specs=pl.BlockSpec((2 * slots, block), lambda g: (0, g)),
        compiler_params=params(16),
    )(rows.reshape(slots, 1), fields)


def potential_kernel(own, parts, fields, *refs):
    chols, out = refs[:parts], refs[parts]
    slots = fields.shape[0] // 2
    devices = slots // own
    unit = SUBLANES // own
    step = chols[0].shape[0]
    pieces = chols[0].shape[1] // LANES
    total = None
    for p in range(parts):
        high, low = split(chols[p][...])
        part = fields[:, p * step : (p + 1) * step]
        value = dot(part, high) + dot(part, low)
        total = value if total is None else total + value
    total = total[:slots] + total[slots:]
    here = pl.program_id(0)
    start = here // unit * (pieces * SUBLANES) + here % unit
    stride = out.shape[0] // devices
    for t in range(pieces):
        for s in range(own):
            at = pl.ds(start + t * SUBLANES + s * unit, devices, stride=stride)
            out[at, :] = total[s * devices : (s + 1) * devices, t * LANES : (t + 1) * LANES]


def potential_tiles(own, fields, chol, orbitals, first, count):
    vectors = chol.shape[0]
    slots = fields.shape[0] // 2
    step = 256
    parts = vectors // step
    rows = slots * count * orbitals // LANES
    return pl.pallas_call(
        functools.partial(potential_kernel, own, parts),
        grid=(count,),
        out_shape=jax.ShapeDtypeStruct((rows, LANES), F32),
        in_specs=[whole(fields.shape)]
        + [pl.BlockSpec((step, orbitals), lambda i, p=p: (p, first + i)) for p in range(parts)],
        out_specs=whole((rows, LANES)),
        compiler_params=params(32),
        cost_estimate=pl.CostEstimate(
            flops=2 * slots * vectors * orbitals * count * 3,
            bytes_accessed=4 * vectors * orbitals * count,
            transcendentals=0,
        ),
    )(fields, *[chol] * parts)


def taylor_kernel(own, chunks, index, gathered, *refs):
    tiles = refs[:chunks]
    out, high, low, term, starts, sems = refs[chunks:]
    orbitals, width = term.shape
    occupied = width // own
    pieces = orbitals // LANES
    devices = tiles[0].shape[0]
    unit = SUBLANES // own
    copies = [
        pltpu.make_async_copy(gathered.at[index[s], pl.ds(0, orbitals)], starts.at[s], sems.at[s]) for s in range(own)
    ]
    for copy in copies:
        copy.start()
    lane = jax.lax.broadcasted_iota(jnp.int32, (1, width), 1) // occupied
    sub = jax.lax.broadcasted_iota(jnp.int32, (SUBLANES, 1), 0) // unit
    for t in range(pieces):
        parts = [tile[...].reshape(devices, -1, pieces, SUBLANES, LANES)[:, :, t] for tile in tiles]
        value_high, value_low = split(jnp.concatenate(parts, axis=1).reshape(-1, LANES))
        high[:, t * LANES : (t + 1) * LANES] = value_high
        low[:, t * LANES : (t + 1) * LANES] = value_low
    for copy in copies:
        copy.wait()
    total = jnp.zeros((orbitals, width), F32)
    for s in range(own):
        source = starts[s]
        inside = index[own + s]
        moved = source
        for shift in range(1, own):
            rolled = pltpu.roll(source, shift * occupied, 1)
            moved = jnp.where((inside + shift) % own == s, rolled, moved)
        total = jnp.where(lane == s, moved, total)
    term[...] = total
    for order in range(1, TERMS):
        term_high, term_low = split(term[...])
        pair = jnp.concatenate([term_high, term_low], axis=1)
        both = dot(high[...], pair)
        value = both[:, :width] + both[:, width:] + dot(low[...], term_high)
        value = value.reshape(-1, own, SUBLANES, width)
        placed = jnp.zeros((value.shape[0], SUBLANES, width), F32)
        for j in range(own):
            for s in range(own):
                shift = ((j - s) * unit) % SUBLANES
                moved = pltpu.roll(value[:, j], shift, 1) if shift else value[:, j]
                placed = jnp.where((sub == j) & (lane == s), moved, placed)
        placed = placed.reshape(orbitals, width) / order
        term[...] = placed
        total = total + placed
    flipped = total.T
    for s in range(own):
        out[s] = flipped[s * occupied : (s + 1) * occupied, :]


def taylor(index, gathered, tiles, own, orbitals, occupied):
    width = own * occupied
    chunks = len(tiles)
    rows = sum(t.shape[0] * t.shape[1] for t in tiles) // (orbitals // LANES)
    vmem = pl.BlockSpec(memory_space=pltpu.VMEM)
    return pl.pallas_call(
        functools.partial(taylor_kernel, own, chunks),
        out_shape=jax.ShapeDtypeStruct((own, occupied, orbitals), F32),
        in_specs=[pl.BlockSpec(memory_space=pltpu.SMEM), pl.BlockSpec(memory_space=pl.ANY)] + [vmem] * chunks,
        out_specs=vmem,
        scratch_shapes=[
            pltpu.VMEM((rows, orbitals), BF16),
            pltpu.VMEM((rows, orbitals), BF16),
            pltpu.VMEM((orbitals, width), F32),
            pltpu.VMEM((own, orbitals, width), F32),
            pltpu.SemaphoreType.DMA((own,)),
        ],
        compiler_params=params(24),
    )(index, gathered, *tiles)


def per_device(trial, walkers, chol, field_noise, log_weight, parent):
    own, orbitals, occupied = walkers.shape
    walk_size = lax.axis_size("walk")
    chol_size = lax.axis_size("chol")
    devices = walk_size * chol_size
    vectors, pairs = chol.shape
    rows_here = pairs // orbitals
    half = rows_here // 2
    place = lax.axis_index(BOTH)

    sent, pack, pair = rotate(
        devices, parent, log_weight, trial.T, walkers.transpose(0, 2, 1), field_noise
    )
    rotated = lax.all_to_all(sent, BOTH, split_axis=0, concat_axis=0, tiled=True)
    gathered = lax.all_gather(pack, "chol", axis=0, tiled=False)
    contracted = contract(pair, chol)
    mine = partial_fields(own, half, place.reshape(1), rotated, contracted, field_noise)
    fields = sum_everywhere(mine, walk_size, chol_size)

    parents = rotated[:, own * half, :own].T.reshape(own * devices).astype(jnp.int32)
    parent_rows = row_of(parents, own, walk_size, chol_size)
    scaled = select(parent_rows, fields)

    unit = SUBLANES // own
    units = rows_here // unit
    cuts = [0] + ([FIRST_UNITS] if units > FIRST_UNITS else []) + [units]
    tiles = []
    for begin, end in zip(cuts[:-1], cuts[1:]):
        chunk = potential_tiles(own, scaled, chol, orbitals, begin * unit, (end - begin) * unit)
        chunk = chunk.reshape(devices, -1, LANES)
        tiles.append(lax.all_to_all(chunk, BOTH, split_axis=0, concat_axis=0, tiled=True))

    local = parent - lax.axis_index("walk") * (own * chol_size)
    source, inside = local // own, local % own
    new_walkers = taylor(
        jnp.concatenate([source, inside]), gathered, tiles, own, orbitals, occupied
    ).transpose(0, 2, 1)

    width = vectors // LANES
    notes = gathered[:, orbitals : orbitals + own * width, :].reshape(own * chol_size, vectors)
    parent_noise = jnp.take(notes, local, axis=0)
    parent_level = jnp.take(gathered[:, -SUBLANES, :own].reshape(own * chol_size), local, axis=0)
    parent_fields = jnp.take(fields, row_of(parent, own, walk_size, chol_size), axis=0)
    shift = parent_noise - parent_fields
    new_log_weight = parent_level + jnp.sum(0.5 * shift * shift - parent_noise * shift, axis=1)
    return (new_walkers, new_log_weight)


def solution(mesh):
    return jax.shard_map(
        per_device,
        mesh=mesh,
        in_specs=(
            P(),
            P(BOTH, None, None),
            P(None, BOTH),
            P(BOTH, None),
            P(BOTH),
            P(BOTH),
        ),
        out_specs=(P(BOTH, None, None), P(BOTH)),
        check_vma=False,
    )
```

```python
import functools

import jax
import jax.numpy as jnp
from jax import lax
from jax.experimental import pallas as pl
from jax.experimental.pallas import tpu as pltpu
from jax.sharding import PartitionSpec as P

TERMS = 6
PRECISE = lax.Precision.HIGHEST
TIME_ROOT = 0.1
BOTH = ("walk", "chol")
LANES = 128
SUBLANES = 8
F32 = jnp.float32
BF16 = jnp.bfloat16
MIB = 1024 * 1024
FIRST_UNITS = 1


def params(mib):
    return pltpu.CompilerParams(vmem_limit_bytes=mib * MIB)


def whole(shape):
    zeros = (0,) * len(shape)
    return pl.BlockSpec(shape, lambda *_: zeros)


def dot(a, b):
    return jnp.dot(a, b, preferred_element_type=F32)


def dot_nt(a, b):
    return lax.dot_general(a, b, (((1,), (1,)), ((), ())), preferred_element_type=F32)


def split(x):
    high = x.astype(BF16)
    low = (x - high.astype(F32)).astype(BF16)
    return high, low


def rotate_kernel(devices, parent, trial, walkers, sent, pair):
    own, occupied, orbitals = walkers.shape
    half = orbitals // devices // 2
    rows = jax.lax.broadcasted_iota(jnp.int32, (occupied, 1), 0)
    state = []
    for s in range(own):
        crossed = lax.dot_general(
            walkers[s], trial[...], (((1,), (1,)), ((), ())), precision=PRECISE, preferred_element_type=F32
        )
        normal = lax.dot_general(
            crossed, crossed, (((1,), (1,)), ((), ())), precision=PRECISE, preferred_element_type=F32
        )
        state.append(jnp.concatenate([normal, crossed], axis=1))
    for k in range(occupied):
        for s in range(own):
            m = state[s]
            pivot = m[k : k + 1, :]
            scaled = pivot / m[k : k + 1, k : k + 1]
            state[s] = jnp.where(rows == k, scaled, m - m[:, k : k + 1] * scaled)
    lane = jax.lax.broadcasted_iota(jnp.int32, (1, LANES), 1)
    packed = jnp.concatenate([walkers[s] for s in range(own)], axis=0).T
    empty = jnp.zeros((occupied, occupied), F32)
    inverse = jnp.concatenate(
        [
            jnp.concatenate([state[s][:, occupied:] if s == c else empty for c in range(own)], axis=1)
            for s in range(own)
        ],
        axis=0,
    )
    rotated = jnp.dot(packed, inverse, precision=PRECISE, preferred_element_type=F32)
    for at, value in ((0, rotated), (own * half, packed)):
        blocks = value.reshape(devices, 2, half, LANES)
        first, second = blocks[:, 0], blocks[:, 1]
        sent[:, at : at + half, :] = jnp.where(lane < occupied, first, pltpu.roll(second, occupied, 2))
        sent[:, at + half : at + 2 * half, :] = jnp.where(lane < occupied, pltpu.roll(first, occupied, 2), second)
    extra = jnp.zeros((SUBLANES, LANES), F32)
    for s in range(own):
        extra = jnp.where(lane == s, parent[s].astype(F32), extra)
    tail = sent.shape[1] - 2 * own * half
    sent[:, 2 * own * half :, :] = jnp.broadcast_to(extra[None, :tail], (devices, tail, LANES))
    value = jnp.concatenate([trial[...]] * 2, axis=0).T
    high, low = split(value)
    pair[...] = jnp.where(lane < occupied, high, low)


def rotate_plain(devices, parent, trial, walkers, sent_rows):
    own, occupied, orbitals = walkers.shape
    half = orbitals // devices // 2
    crossed = jnp.einsum("wkm,nm->wkn", walkers, trial, precision=PRECISE)
    normal = jnp.einsum("wkn,wln->wkl", crossed, crossed, precision=PRECISE)
    factor = jnp.linalg.cholesky(normal)
    inverse = jax.vmap(lambda f, c: jax.scipy.linalg.cho_solve((f, True), c))(factor, crossed)
    rotated = jnp.einsum("wkm,wkn->wmn", walkers, inverse, precision=PRECISE)
    sent = jnp.concatenate([rotated, walkers.transpose(0, 2, 1)], axis=0)
    sent = sent.reshape(2 * own, devices, 2, half, occupied).transpose(1, 0, 3, 2, 4)
    sent = sent.reshape(devices, 2 * own * half, 2 * occupied)
    extra = jnp.zeros((sent_rows - 2 * own * half, LANES), F32).at[0, :own].set(parent.astype(F32))
    sent = jnp.concatenate([sent, jnp.broadcast_to(extra[None], (devices,) + extra.shape)], axis=1)
    return sent, jnp.concatenate(split(trial.T), axis=1)


def eights(rows):
    return -(-rows // SUBLANES) * SUBLANES


def rotate(devices, parent, trial, walkers):
    own, occupied, orbitals = walkers.shape
    half = orbitals // devices // 2
    sent_rows = eights(2 * own * half + 1)
    if half % SUBLANES or own != 2 or own * occupied != LANES:
        return rotate_plain(devices, parent, trial, walkers, sent_rows)
    return pl.pallas_call(
        functools.partial(rotate_kernel, devices),
        grid=(1,),
        out_shape=(
            jax.ShapeDtypeStruct((devices, sent_rows, LANES), F32),
            jax.ShapeDtypeStruct((orbitals, 2 * occupied), BF16),
        ),
        in_specs=[pl.BlockSpec(memory_space=pltpu.SMEM), whole(trial.shape), whole(walkers.shape)],
        out_specs=(whole((devices, sent_rows, LANES)), whole((orbitals, 2 * occupied))),
        compiler_params=params(16),
    )(parent, trial, walkers)


def contract_kernel(pair, chol, out):
    orbitals = pair.shape[0]
    occupied = pair.shape[1] // 2
    half = chol.shape[1] // orbitals // 2
    lane = jax.lax.broadcasted_iota(jnp.int32, (1, 2 * occupied), 1)
    both_parts = pair[...]
    alone = jnp.where(lane < occupied, both_parts, jnp.zeros_like(both_parts))

    def one(i):
        chol_high, chol_low = split(chol[:, i * orbitals : (i + 1) * orbitals])
        both = dot(chol_high, both_parts) + dot(chol_low, alone)
        return both + pltpu.roll(both, occupied, 1)

    for i in range(half):
        out[:, i * 2 * occupied : (i + 1) * 2 * occupied] = jnp.where(lane < occupied, one(i), one(i + half))


def contract(pair, chol):
    vectors, pairs = chol.shape
    orbitals, occupied = pair.shape[0], pair.shape[1] // 2
    columns = pairs // orbitals * occupied
    block = 256
    return pl.pallas_call(
        contract_kernel,
        grid=(vectors // block,),
        out_shape=jax.ShapeDtypeStruct((vectors, columns), F32),
        in_specs=[whole(pair.shape), pl.BlockSpec((block, pairs), lambda g: (g, 0))],
        out_specs=pl.BlockSpec((block, columns), lambda g: (g, 0)),
        compiler_params=params(48),
        cost_estimate=pl.CostEstimate(
            flops=2 * vectors * pairs * occupied * 3, bytes_accessed=4 * vectors * (pairs + columns), transcendentals=0
        ),
    )(pair, chol)


def bias_kernel(own, half, place, rotated, contracted, noise, out, stacked):
    devices = rotated.shape[0]
    slots = own * devices

    @pl.when(pl.program_id(0) == 0)
    def _():
        for i in range(half):
            for s in range(own):
                high, low = split(rotated[:, s * half + i, :])
                at = s * devices
                stacked[at : at + devices, i * LANES : (i + 1) * LANES] = high
                stacked[slots + at : slots + at + devices, i * LANES : (i + 1) * LANES] = low

    b_high, b_low = split(contracted[...])
    both = dot_nt(stacked[...], b_high) + dot_nt(stacked[...], b_low)
    value = -TIME_ROOT * (both[:slots] + both[slots:])
    rows = jax.lax.broadcasted_iota(jnp.int32, (slots, 1), 0)
    for s in range(own):
        value += jnp.where(rows == s * devices + place[0], noise[s : s + 1, :], 0.0)
    out[...] = value


def partial_fields(own, half, place, rotated, contracted, noise):
    vectors, columns = contracted.shape
    devices = rotated.shape[0]
    block = 512
    return pl.pallas_call(
        functools.partial(bias_kernel, own, half),
        grid=(vectors // block,),
        out_shape=jax.ShapeDtypeStruct((own * devices, vectors), F32),
        in_specs=[
            pl.BlockSpec(memory_space=pltpu.SMEM),
            whole(rotated.shape),
            pl.BlockSpec((block, columns), lambda g: (g, 0)),
            pl.BlockSpec((own, block), lambda g: (0, g)),
        ],
        out_specs=pl.BlockSpec((own * devices, block), lambda g: (0, g)),
        scratch_shapes=[pltpu.VMEM((2 * own * devices, columns), BF16)],
        compiler_params=params(48),
    )(place, rotated, contracted, noise)


def send(x, walk_size, chol_size, target):
    return lax.ppermute(x, BOTH, [(i, target(i)) for i in range(walk_size * chol_size)])


def sum_everywhere(x, walk_size, chol_size):
    walk = lax.axis_index("walk")
    core = lax.axis_index("chol") % 2
    half = x.shape[0] // 2
    quarter = half // walk_size
    mine = lax.dynamic_slice_in_dim(x, core * half, half, 0)
    other = lax.dynamic_slice_in_dim(x, (1 - core) * half, half, 0)
    chip = mine + send(other, walk_size, chol_size, lambda i: i ^ 1)
    total = lax.dynamic_slice_in_dim(chip, walk * quarter, quarter, 0)
    got = [
        send(
            lax.dynamic_slice_in_dim(chip, (walk ^ r) * quarter, quarter, 0),
            walk_size, chol_size, lambda i, r=r: i ^ (r * chol_size),
        )
        for r in range(1, walk_size)
    ]
    for g in got:
        total = total + g
    got = [send(total, walk_size, chol_size, lambda i, r=r: i ^ (2 * r)) for r in range(1, chol_size // 2)]
    for g in got:
        total = total + g
    blocks = [total] + [
        send(total, walk_size, chol_size, lambda i, r=r: i ^ (r * chol_size)) for r in range(1, walk_size)
    ]
    here = jnp.concatenate(blocks, axis=0)
    there = send(here, walk_size, chol_size, lambda i: i ^ 1)
    return jnp.concatenate([here, there], axis=0)


def row_of(walker, own, walk_size, chol_size):
    everyone = own * walk_size * chol_size
    walk = lax.axis_index("walk")
    core = lax.axis_index("chol") % 2
    row = (walker % own) * (walk_size * chol_size) + walker // own
    half = everyone // 2
    quarter = half // walk_size
    inside = row % half
    return ((row // half) ^ core) * half + ((inside // quarter) ^ walk) * quarter + inside % quarter


def select_kernel(rows, fields, out):
    slots = fields.shape[0]
    lane = jax.lax.broadcasted_iota(jnp.int32, (slots, slots), 1)
    pick = jnp.where(lane == rows[...], 1.0, 0.0).astype(BF16)
    value = fields[...]
    first, rest = split(value)
    second, third = split(value - first.astype(F32))
    picked = dot(pick, first) + dot(pick, second) + dot(pick, third)
    high, low = split(TIME_ROOT * picked)
    out[:slots, :] = high
    out[slots:, :] = low


def select(rows, fields):
    slots, vectors = fields.shape
    block = 512
    return pl.pallas_call(
        select_kernel,
        grid=(vectors // block,),
        out_shape=jax.ShapeDtypeStruct((2 * slots, vectors), BF16),
        in_specs=[whole((slots, 1)), pl.BlockSpec((slots, block), lambda g: (0, g))],
        out_specs=pl.BlockSpec((2 * slots, block), lambda g: (0, g)),
        compiler_params=params(16),
    )(rows.reshape(slots, 1), fields)


def carry_kernel(own, half, rows, received, out):
    devices = received.shape[0]
    slots = own * devices
    lane = jax.lax.broadcasted_iota(jnp.int32, (slots, slots), 1)
    pick = jnp.where(lane == rows[...], 1.0, 0.0).astype(BF16)
    for i in range(half):
        value = jnp.concatenate([received[:, (own + s) * half + i, :] for s in range(own)], axis=0)
        first, rest = split(value)
        second, third = split(value - first.astype(F32))
        picked = dot(pick, first) + dot(pick, second) + dot(pick, third)
        for s in range(own):
            out[s * half + i] = picked[s * devices : (s + 1) * devices]


def carry(own, half, rows, received):
    devices = received.shape[0]
    shape = (own * half, devices, LANES)
    return pl.pallas_call(
        functools.partial(carry_kernel, own, half),
        grid=(1,),
        out_shape=jax.ShapeDtypeStruct(shape, F32),
        in_specs=[whole((own * devices, 1)), whole(received.shape)],
        out_specs=whole(shape),
        compiler_params=params(16),
    )(rows.reshape(-1, 1), received)


def potential_kernel(own, parts, base, fields, *refs):
    chols, out = refs[:parts], refs[-1]
    slots = fields.shape[0] // 2
    devices = slots // own
    unit = SUBLANES // own
    step = chols[0].shape[0]
    pieces = chols[0].shape[1] // LANES
    total = None
    for p in range(parts):
        high, low = split(chols[p][...])
        part = fields[:, p * step : (p + 1) * step]
        value = dot(part, high) + dot(part, low)
        total = value if total is None else total + value
    total = total[:slots] + total[slots:]
    here = pl.program_id(0)
    start = here // unit * (pieces * SUBLANES) + here % unit
    stride = out.shape[0] // devices
    for t in range(pieces):
        for s in range(own):
            at = pl.ds(start + t * SUBLANES + s * unit, devices, stride=stride)
            out[at, :] = total[s * devices : (s + 1) * devices, t * LANES : (t + 1) * LANES]
    if len(refs) == parts + 1:
        return
    orbital_rows, summed, noise, places, levels = refs[parts:-1]

    @pl.when(here == 0)
    def _():
        lane = jax.lax.broadcasted_iota(jnp.int32, (1, LANES), 1)
        line = jnp.zeros((1, LANES), F32)
        for s in range(own):
            shift = noise[s : s + 1, :] - summed[pl.ds(places[s], 1), :]
            terms = 0.5 * shift * shift - noise[s : s + 1, :] * shift
            line = jnp.where(lane == s, levels[s] + jnp.sum(terms, axis=1, keepdims=True), line)
        taken = orbital_rows.shape[0]
        for r in range(taken):
            out[pl.ds(base + r, devices, stride=stride), :] = orbital_rows[r]
        for r in range(taken, stride - base):
            out[pl.ds(base + r, devices, stride=stride), :] = jnp.broadcast_to(line, (devices, LANES))


def potential_tiles(own, fields, chol, orbitals, first, count, along):
    vectors = chol.shape[0]
    slots = fields.shape[0] // 2
    step = 256
    parts = vectors // step
    devices = slots // own
    base = own * count * orbitals // LANES
    rows = devices * base
    smem = pl.BlockSpec(memory_space=pltpu.SMEM)
    more = []
    if along:
        rows += devices * eights(along[0].shape[0] + 1)
        more = [whole(a.shape) for a in along[:3]] + [smem, smem]
    return pl.pallas_call(
        functools.partial(potential_kernel, own, parts, base),
        grid=(count,),
        out_shape=jax.ShapeDtypeStruct((rows, LANES), F32),
        in_specs=[whole(fields.shape)]
        + [pl.BlockSpec((step, orbitals), lambda i, p=p: (p, first + i)) for p in range(parts)]
        + more,
        out_specs=whole((rows, LANES)),
        compiler_params=params(32),
        cost_estimate=pl.CostEstimate(
            flops=2 * slots * vectors * orbitals * count * 3,
            bytes_accessed=4 * vectors * orbitals * count,
            transcendentals=0,
        ),
    )(fields, *[chol] * parts, *along)


def taylor_kernel(own, chunks, base, *refs):
    tiles = refs[:chunks]
    begin = refs[chunks:-4]
    out, high, low, term = refs[-4:]
    orbitals, width = term.shape
    occupied = width // own
    pieces = orbitals // LANES
    devices = tiles[0].shape[0]
    half = orbitals // devices // 2
    unit = SUBLANES // own
    lane = jax.lax.broadcasted_iota(jnp.int32, (1, width), 1) // occupied
    sub = jax.lax.broadcasted_iota(jnp.int32, (SUBLANES, 1), 0) // unit
    for t in range(pieces):
        parts = []
        for c, tile in enumerate(tiles):
            value = tile[:, :base, :] if c == 0 else tile[...]
            parts.append(value.reshape(devices, -1, pieces, SUBLANES, LANES)[:, :, t])
        value_high, value_low = split(jnp.concatenate(parts, axis=1).reshape(-1, LANES))
        high[:, t * LANES : (t + 1) * LANES] = value_high
        low[:, t * LANES : (t + 1) * LANES] = value_low
    if begin:
        total = begin[0][...]
    else:
        left = tiles[0][:, base : base + half, :]
        right = tiles[0][:, base + half : base + 2 * half, :]
        upper = jnp.where(lane == 0, left, pltpu.roll(right, occupied, 2))
        lower = jnp.where(lane == 0, pltpu.roll(left, occupied, 2), right)
        total = jnp.stack([upper, lower], axis=1).reshape(orbitals, width)
    term[...] = total
    for order in range(1, TERMS):
        term_high, term_low = split(term[...])
        pair = jnp.concatenate([term_high, term_low], axis=1)
        both = dot(high[...], pair)
        value = both[:, :width] + both[:, width:] + dot(low[...], term_high)
        value = value.reshape(-1, own, SUBLANES, width)
        placed = jnp.zeros((value.shape[0], SUBLANES, width), F32)
        for j in range(own):
            for s in range(own):
                shift = ((j - s) * unit) % SUBLANES
                moved = pltpu.roll(value[:, j], shift, 1) if shift else value[:, j]
                placed = jnp.where((sub == j) & (lane == s), moved, placed)
        placed = placed.reshape(orbitals, width) / order
        term[...] = placed
        total = total + placed
    flipped = total.T
    for s in range(own):
        out[s] = flipped[s * occupied : (s + 1) * occupied, :]


def taylor(tiles, base, own, orbitals, occupied):
    width = own * occupied
    chunks = len(tiles)
    devices = tiles[0].shape[0]
    half = orbitals // devices // 2
    begin = []
    if half % SUBLANES or own != 2:
        start = tiles[0][:, base : base + own * half].reshape(devices, own, half, 2, occupied)
        begin = [start.transpose(0, 3, 2, 1, 4).reshape(orbitals, width)]
    vmem = pl.BlockSpec(memory_space=pltpu.VMEM)
    return pl.pallas_call(
        functools.partial(taylor_kernel, own, chunks, base),
        out_shape=jax.ShapeDtypeStruct((own, occupied, orbitals), F32),
        in_specs=[vmem] * (chunks + len(begin)),
        out_specs=vmem,
        scratch_shapes=[
            pltpu.VMEM((own * orbitals, orbitals), BF16),
            pltpu.VMEM((own * orbitals, orbitals), BF16),
            pltpu.VMEM((orbitals, width), F32),
        ],
        compiler_params=params(24),
    )(*tiles, *begin)


def per_device(trial, walkers, chol, field_noise, log_weight, parent):
    own, orbitals, occupied = walkers.shape
    walk_size = lax.axis_size("walk")
    chol_size = lax.axis_size("chol")
    devices = walk_size * chol_size
    vectors, pairs = chol.shape
    rows_here = pairs // orbitals
    half = rows_here // 2
    place = lax.axis_index(BOTH)

    sent, pair = rotate(devices, parent, trial.T, walkers.transpose(0, 2, 1))
    rotated = lax.all_to_all(sent, BOTH, split_axis=0, concat_axis=0, tiled=True)
    contracted = contract(pair, chol)
    mine = partial_fields(own, half, place.reshape(1), rotated, contracted, field_noise)
    fields = sum_everywhere(mine, walk_size, chol_size)

    parents = rotated[:, 2 * own * half, :own].T.reshape(own * devices).astype(jnp.int32)
    orbital_rows = carry(own, half, (parents % own) * devices + parents // own, rotated)
    scaled = select(row_of(parents, own, walk_size, chol_size), fields)
    places = row_of(place * own + jnp.arange(own, dtype=jnp.int32), own, walk_size, chol_size)

    unit = SUBLANES // own
    units = rows_here // unit
    cuts = [0] + ([FIRST_UNITS] if units > FIRST_UNITS else []) + [units]
    tiles = []
    for begin, end in zip(cuts[:-1], cuts[1:]):
        along = () if begin else (orbital_rows, fields, field_noise, places, log_weight)
        chunk = potential_tiles(own, scaled, chol, orbitals, begin * unit, (end - begin) * unit, along)
        chunk = chunk.reshape(devices, -1, LANES)
        tiles.append(lax.all_to_all(chunk, BOTH, split_axis=0, concat_axis=0, tiled=True))

    base = own * cuts[1] * unit * orbitals // LANES
    new_walkers = taylor(tiles, base, own, orbitals, occupied).transpose(0, 2, 1)
    new_log_weight = tiles[0][parent // own, base + own * half, parent % own]
    return (new_walkers, new_log_weight)


def solution(mesh):
    return jax.shard_map(
        per_device,
        mesh=mesh,
        in_specs=(
            P(),
            P(BOTH, None, None),
            P(None, BOTH),
            P(BOTH, None),
            P(BOTH),
            P(BOTH),
        ),
        out_specs=(P(BOTH, None, None), P(BOTH)),
        check_vma=False,
    )
```

```python
import functools

import jax
import jax.numpy as jnp
from jax import lax
from jax.experimental import pallas as pl
from jax.experimental.pallas import tpu as pltpu
from jax.sharding import PartitionSpec as P

TERMS = 6
PRECISE = lax.Precision.HIGHEST
TIME_ROOT = 0.1
BOTH = ("walk", "chol")
LANES = 128
SUBLANES = 8
F32 = jnp.float32
BF16 = jnp.bfloat16
MIB = 1024 * 1024
FIRST_UNITS = 1
HEAD = 512
PIECE = 128


def params(mib):
    return pltpu.CompilerParams(vmem_limit_bytes=mib * MIB)


def whole(shape):
    zeros = (0,) * len(shape)
    return pl.BlockSpec(shape, lambda *_: zeros)


def dot(a, b):
    return jnp.dot(a, b, preferred_element_type=F32)


def dot_nt(a, b):
    return lax.dot_general(a, b, (((1,), (1,)), ((), ())), preferred_element_type=F32)


def split(x):
    high = x.astype(BF16)
    low = (x - high.astype(F32)).astype(BF16)
    return high, low


def rotate_kernel(devices, parent, trial_in, walkers_in, chol, sent, pair, contracted, trial, walkers, loaded, done, sems):
    own, occupied, orbitals = walkers.shape
    half = orbitals // devices // 2
    count = loaded.shape[0] // PIECE
    small = [
        pltpu.make_async_copy(walkers_in, walkers, sems.at[0]),
        pltpu.make_async_copy(trial_in, trial, sems.at[1]),
    ]
    reads, writes = [], []
    for p in range(count):
        at = pl.ds(p * PIECE, PIECE)
        reads.append(pltpu.make_async_copy(chol.at[at], loaded.at[at], sems.at[2 + p]))
        writes.append(pltpu.make_async_copy(done.at[at], contracted.at[at], sems.at[2 + count + p]))
    for copy in small + reads:
        copy.start()
    for copy in small:
        copy.wait()
    lane = jax.lax.broadcasted_iota(jnp.int32, (1, LANES), 1)
    both_parts = jnp.concatenate([trial[...]] * 2, axis=0).T
    high, low = split(both_parts)
    both_parts = jnp.where(lane < occupied, high, low)
    pair[...] = both_parts
    alone = jnp.where(lane < occupied, both_parts, jnp.zeros_like(both_parts))
    rows = jax.lax.broadcasted_iota(jnp.int32, (occupied, 1), 0)
    state = []
    for s in range(own):
        crossed = lax.dot_general(
            walkers[s], trial[...], (((1,), (1,)), ((), ())), precision=PRECISE, preferred_element_type=F32
        )
        normal = lax.dot_general(
            crossed, crossed, (((1,), (1,)), ((), ())), precision=PRECISE, preferred_element_type=F32
        )
        state.append(jnp.concatenate([normal, crossed], axis=1))

    def eliminate(k):
        for s in range(own):
            m = state[s]
            pivot = m[k : k + 1, :]
            scaled = pivot / m[k : k + 1, k : k + 1]
            state[s] = jnp.where(rows == k, scaled, m - m[:, k : k + 1] * scaled)

    pivots = 0
    for p in range(count):
        reads[p].wait()
        at = slice(p * PIECE, (p + 1) * PIECE)
        for i in range(half):
            ends = [contract_row(loaded[at, r * orbitals : (r + 1) * orbitals], both_parts, alone) for r in (i, i + half)]
            done[at, i * LANES : (i + 1) * LANES] = jnp.where(lane < occupied, ends[0], ends[1])
            upto = occupied * (p * half + i + 1) // (count * half)
            for k in range(pivots, upto):
                eliminate(k)
            pivots = upto
        writes[p].start()
    packed = jnp.concatenate([walkers[s] for s in range(own)], axis=0).T
    empty = jnp.zeros((occupied, occupied), F32)
    inverse = jnp.concatenate(
        [
            jnp.concatenate([state[s][:, occupied:] if s == c else empty for c in range(own)], axis=1)
            for s in range(own)
        ],
        axis=0,
    )
    rotated = jnp.dot(packed, inverse, precision=PRECISE, preferred_element_type=F32)
    for at, value in ((0, rotated), (own * half, packed)):
        blocks = value.reshape(devices, 2, half, LANES)
        first, second = blocks[:, 0], blocks[:, 1]
        sent[:, at : at + half, :] = jnp.where(lane < occupied, first, pltpu.roll(second, occupied, 2))
        sent[:, at + half : at + 2 * half, :] = jnp.where(lane < occupied, pltpu.roll(first, occupied, 2), second)
    extra = jnp.zeros((SUBLANES, LANES), F32)
    for s in range(own):
        extra = jnp.where(lane == s, parent[s].astype(F32), extra)
    tail = sent.shape[1] - 2 * own * half
    sent[:, 2 * own * half :, :] = jnp.broadcast_to(extra[None, :tail], (devices, tail, LANES))
    for copy in writes:
        copy.wait()


def rotate_plain(devices, parent, trial, walkers, sent_rows):
    own, occupied, orbitals = walkers.shape
    half = orbitals // devices // 2
    crossed = jnp.einsum("wkm,nm->wkn", walkers, trial, precision=PRECISE)
    normal = jnp.einsum("wkn,wln->wkl", crossed, crossed, precision=PRECISE)
    factor = jnp.linalg.cholesky(normal)
    inverse = jax.vmap(lambda f, c: jax.scipy.linalg.cho_solve((f, True), c))(factor, crossed)
    rotated = jnp.einsum("wkm,wkn->wmn", walkers, inverse, precision=PRECISE)
    sent = jnp.concatenate([rotated, walkers.transpose(0, 2, 1)], axis=0)
    sent = sent.reshape(2 * own, devices, 2, half, occupied).transpose(1, 0, 3, 2, 4)
    sent = sent.reshape(devices, 2 * own * half, 2 * occupied)
    extra = jnp.zeros((sent_rows - 2 * own * half, LANES), F32).at[0, :own].set(parent.astype(F32))
    sent = jnp.concatenate([sent, jnp.broadcast_to(extra[None], (devices,) + extra.shape)], axis=1)
    return sent, jnp.concatenate(split(trial.T), axis=1)


def eights(rows):
    return -(-rows // SUBLANES) * SUBLANES


def rotate(devices, parent, trial, walkers, chol):
    own, occupied, orbitals = walkers.shape
    vectors = chol.shape[0]
    columns = chol.shape[1] // orbitals * occupied
    half = orbitals // devices // 2
    sent_rows = eights(2 * own * half + 1)
    if half % SUBLANES or own != 2 or own * occupied != LANES:
        return rotate_plain(devices, parent, trial, walkers, sent_rows) + (None,)
    anywhere = pl.BlockSpec(memory_space=pl.ANY)
    return pl.pallas_call(
        functools.partial(rotate_kernel, devices),
        grid=(1,),
        out_shape=(
            jax.ShapeDtypeStruct((devices, sent_rows, LANES), F32),
            jax.ShapeDtypeStruct((orbitals, 2 * occupied), BF16),
            jax.ShapeDtypeStruct((vectors, columns), F32),
        ),
        in_specs=[pl.BlockSpec(memory_space=pltpu.SMEM), anywhere, anywhere, anywhere],
        out_specs=(whole((devices, sent_rows, LANES)), whole((orbitals, 2 * occupied)), anywhere),
        scratch_shapes=[
            pltpu.VMEM(trial.shape, F32),
            pltpu.VMEM(walkers.shape, F32),
            pltpu.VMEM((HEAD, chol.shape[1]), F32),
            pltpu.VMEM((HEAD, columns), F32),
            pltpu.SemaphoreType.DMA((2 + 2 * (HEAD // PIECE),)),
        ],
        compiler_params=params(60),
    )(parent, trial, walkers, chol)


def contract_row(part, both_parts, alone):
    chol_high, chol_low = split(part)
    both = dot(chol_high, both_parts) + dot(chol_low, alone)
    return both + pltpu.roll(both, both.shape[1] // 2, 1)


def contract_kernel(pair, chol, *refs):
    out = refs[-1]
    orbitals = pair.shape[0]
    occupied = pair.shape[1] // 2
    half = chol.shape[1] // orbitals // 2
    lane = jax.lax.broadcasted_iota(jnp.int32, (1, 2 * occupied), 1)
    both_parts = pair[...]
    alone = jnp.where(lane < occupied, both_parts, jnp.zeros_like(both_parts))
    for i in range(half):
        ends = [contract_row(chol[:, r * orbitals : (r + 1) * orbitals], both_parts, alone) for r in (i, i + half)]
        out[:, i * 2 * occupied : (i + 1) * 2 * occupied] = jnp.where(lane < occupied, ends[0], ends[1])


def contract(pair, chol, begun):
    vectors, pairs = chol.shape
    orbitals, occupied = pair.shape[0], pair.shape[1] // 2
    columns = pairs // orbitals * occupied
    block = 256
    skip = 0 if begun is None else HEAD // block
    more = [] if begun is None else [begun]
    rest = vectors - skip * block
    return pl.pallas_call(
        contract_kernel,
        grid=(rest // block,),
        out_shape=jax.ShapeDtypeStruct((vectors, columns), F32),
        in_specs=[whole(pair.shape), pl.BlockSpec((block, pairs), lambda g: (g + skip, 0))]
        + [pl.BlockSpec(memory_space=pl.ANY)] * len(more),
        out_specs=pl.BlockSpec((block, columns), lambda g: (g + skip, 0)),
        input_output_aliases={2: 0} if more else {},
        compiler_params=params(48),
        cost_estimate=pl.CostEstimate(
            flops=2 * rest * pairs * occupied * 3, bytes_accessed=4 * rest * (pairs + columns), transcendentals=0
        ),
    )(pair, chol, *more)


def bias_kernel(own, half, place, rotated, contracted, noise, out, stacked):
    devices = rotated.shape[0]
    slots = own * devices

    @pl.when(pl.program_id(0) == 0)
    def _():
        for i in range(half):
            for s in range(own):
                high, low = split(rotated[:, s * half + i, :])
                at = s * devices
                stacked[at : at + devices, i * LANES : (i + 1) * LANES] = high
                stacked[slots + at : slots + at + devices, i * LANES : (i + 1) * LANES] = low

    b_high, b_low = split(contracted[...])
    both = dot_nt(stacked[...], b_high) + dot_nt(stacked[...], b_low)
    value = -TIME_ROOT * (both[:slots] + both[slots:])
    rows = jax.lax.broadcasted_iota(jnp.int32, (slots, 1), 0)
    for s in range(own):
        value += jnp.where(rows == s * devices + place[0], noise[s : s + 1, :], 0.0)
    out[...] = value


def partial_fields(own, half, place, rotated, contracted, noise):
    vectors, columns = contracted.shape
    devices = rotated.shape[0]
    block = 512
    return pl.pallas_call(
        functools.partial(bias_kernel, own, half),
        grid=(vectors // block,),
        out_shape=jax.ShapeDtypeStruct((own * devices, vectors), F32),
        in_specs=[
            pl.BlockSpec(memory_space=pltpu.SMEM),
            whole(rotated.shape),
            pl.BlockSpec((block, columns), lambda g: (g, 0)),
            pl.BlockSpec((own, block), lambda g: (0, g)),
        ],
        out_specs=pl.BlockSpec((own * devices, block), lambda g: (0, g)),
        scratch_shapes=[pltpu.VMEM((2 * own * devices, columns), BF16)],
        compiler_params=params(48),
    )(place, rotated, contracted, noise)


def send(x, walk_size, chol_size, target):
    return lax.ppermute(x, BOTH, [(i, target(i)) for i in range(walk_size * chol_size)])


def sum_everywhere(x, walk_size, chol_size):
    walk = lax.axis_index("walk")
    core = lax.axis_index("chol") % 2
    half = x.shape[0] // 2
    quarter = half // walk_size
    mine = lax.dynamic_slice_in_dim(x, core * half, half, 0)
    other = lax.dynamic_slice_in_dim(x, (1 - core) * half, half, 0)
    chip = mine + send(other, walk_size, chol_size, lambda i: i ^ 1)
    total = lax.dynamic_slice_in_dim(chip, walk * quarter, quarter, 0)
    got = [
        send(
            lax.dynamic_slice_in_dim(chip, (walk ^ r) * quarter, quarter, 0),
            walk_size, chol_size, lambda i, r=r: i ^ (r * chol_size),
        )
        for r in range(1, walk_size)
    ]
    for g in got:
        total = total + g
    got = [send(total, walk_size, chol_size, lambda i, r=r: i ^ (2 * r)) for r in range(1, chol_size // 2)]
    for g in got:
        total = total + g
    blocks = [total] + [
        send(total, walk_size, chol_size, lambda i, r=r: i ^ (r * chol_size)) for r in range(1, walk_size)
    ]
    here = jnp.concatenate(blocks, axis=0)
    there = send(here, walk_size, chol_size, lambda i: i ^ 1)
    return jnp.concatenate([here, there], axis=0)


def row_of(walker, own, walk_size, chol_size):
    everyone = own * walk_size * chol_size
    walk = lax.axis_index("walk")
    core = lax.axis_index("chol") % 2
    row = (walker % own) * (walk_size * chol_size) + walker // own
    half = everyone // 2
    quarter = half // walk_size
    inside = row % half
    return ((row // half) ^ core) * half + ((inside // quarter) ^ walk) * quarter + inside % quarter


def select_kernel(rows, fields, out):
    slots = fields.shape[0]
    lane = jax.lax.broadcasted_iota(jnp.int32, (slots, slots), 1)
    pick = jnp.where(lane == rows[...], 1.0, 0.0).astype(BF16)
    value = fields[...]
    first, rest = split(value)
    second, third = split(value - first.astype(F32))
    picked = dot(pick, first) + dot(pick, second) + dot(pick, third)
    high, low = split(TIME_ROOT * picked)
    out[:slots, :] = high
    out[slots:, :] = low


def select(rows, fields):
    slots, vectors = fields.shape
    block = 512
    return pl.pallas_call(
        select_kernel,
        grid=(vectors // block,),
        out_shape=jax.ShapeDtypeStruct((2 * slots, vectors), BF16),
        in_specs=[whole((slots, 1)), pl.BlockSpec((slots, block), lambda g: (0, g))],
        out_specs=pl.BlockSpec((2 * slots, block), lambda g: (0, g)),
        compiler_params=params(16),
    )(rows.reshape(slots, 1), fields)


def carry_kernel(own, half, rows, received, out):
    devices = received.shape[0]
    slots = own * devices
    lane = jax.lax.broadcasted_iota(jnp.int32, (slots, slots), 1)
    pick = jnp.where(lane == rows[...], 1.0, 0.0).astype(BF16)
    for i in range(half):
        value = jnp.concatenate([received[:, (own + s) * half + i, :] for s in range(own)], axis=0)
        first, rest = split(value)
        second, third = split(value - first.astype(F32))
        picked = dot(pick, first) + dot(pick, second) + dot(pick, third)
        for s in range(own):
            out[s * half + i] = picked[s * devices : (s + 1) * devices]


def carry(own, half, rows, received):
    devices = received.shape[0]
    shape = (own * half, devices, LANES)
    return pl.pallas_call(
        functools.partial(carry_kernel, own, half),
        grid=(1,),
        out_shape=jax.ShapeDtypeStruct(shape, F32),
        in_specs=[whole((own * devices, 1)), whole(received.shape)],
        out_specs=whole(shape),
        compiler_params=params(16),
    )(rows.reshape(-1, 1), received)


def potential_kernel(own, parts, base, fields, *refs):
    chols, out = refs[:parts], refs[-1]
    slots = fields.shape[0] // 2
    devices = slots // own
    unit = SUBLANES // own
    step = chols[0].shape[0]
    pieces = chols[0].shape[1] // LANES
    total = None
    for p in range(parts):
        high, low = split(chols[p][...])
        part = fields[:, p * step : (p + 1) * step]
        value = dot(part, high) + dot(part, low)
        total = value if total is None else total + value
    total = total[:slots] + total[slots:]
    here = pl.program_id(0)
    start = here // unit * (pieces * SUBLANES) + here % unit
    stride = out.shape[0] // devices
    for t in range(pieces):
        for s in range(own):
            at = pl.ds(start + t * SUBLANES + s * unit, devices, stride=stride)
            out[at, :] = total[s * devices : (s + 1) * devices, t * LANES : (t + 1) * LANES]
    if len(refs) == parts + 1:
        return
    orbital_rows, summed, noise, places, levels = refs[parts:-1]

    @pl.when(here == 0)
    def _():
        lane = jax.lax.broadcasted_iota(jnp.int32, (1, LANES), 1)
        line = jnp.zeros((1, LANES), F32)
        for s in range(own):
            shift = noise[s : s + 1, :] - summed[pl.ds(places[s], 1), :]
            terms = 0.5 * shift * shift - noise[s : s + 1, :] * shift
            line = jnp.where(lane == s, levels[s] + jnp.sum(terms, axis=1, keepdims=True), line)
        taken = orbital_rows.shape[0]
        for r in range(taken):
            out[pl.ds(base + r, devices, stride=stride), :] = orbital_rows[r]
        for r in range(taken, stride - base):
            out[pl.ds(base + r, devices, stride=stride), :] = jnp.broadcast_to(line, (devices, LANES))


def potential_tiles(own, fields, chol, orbitals, first, count, along):
    vectors = chol.shape[0]
    slots = fields.shape[0] // 2
    step = 256
    parts = vectors // step
    devices = slots // own
    base = own * count * orbitals // LANES
    rows = devices * base
    smem = pl.BlockSpec(memory_space=pltpu.SMEM)
    more = []
    if along:
        rows += devices * eights(along[0].shape[0] + 1)
        more = [whole(a.shape) for a in along[:3]] + [smem, smem]
    return pl.pallas_call(
        functools.partial(potential_kernel, own, parts, base),
        grid=(count,),
        out_shape=jax.ShapeDtypeStruct((rows, LANES), F32),
        in_specs=[whole(fields.shape)]
        + [pl.BlockSpec((step, orbitals), lambda i, p=p: (p, first + i)) for p in range(parts)]
        + more,
        out_specs=whole((rows, LANES)),
        compiler_params=params(32),
        cost_estimate=pl.CostEstimate(
            flops=2 * slots * vectors * orbitals * count * 3,
            bytes_accessed=4 * vectors * orbitals * count,
            transcendentals=0,
        ),
    )(fields, *[chol] * parts, *along)


def taylor_kernel(own, chunks, base, *refs):
    tiles = refs[:chunks]
    begin = refs[chunks:-4]
    out, high, low, term = refs[-4:]
    orbitals, width = term.shape
    occupied = width // own
    pieces = orbitals // LANES
    devices = tiles[0].shape[0]
    half = orbitals // devices // 2
    unit = SUBLANES // own
    lane = jax.lax.broadcasted_iota(jnp.int32, (1, width), 1) // occupied
    sub = jax.lax.broadcasted_iota(jnp.int32, (SUBLANES, 1), 0) // unit
    for t in range(pieces):
        parts = []
        for c, tile in enumerate(tiles):
            value = tile[:, :base, :] if c == 0 else tile[...]
            parts.append(value.reshape(devices, -1, pieces, SUBLANES, LANES)[:, :, t])
        value_high, value_low = split(jnp.concatenate(parts, axis=1).reshape(-1, LANES))
        high[:, t * LANES : (t + 1) * LANES] = value_high
        low[:, t * LANES : (t + 1) * LANES] = value_low
    if begin:
        total = begin[0][...]
    else:
        left = tiles[0][:, base : base + half, :]
        right = tiles[0][:, base + half : base + 2 * half, :]
        upper = jnp.where(lane == 0, left, pltpu.roll(right, occupied, 2))
        lower = jnp.where(lane == 0, pltpu.roll(left, occupied, 2), right)
        total = jnp.stack([upper, lower], axis=1).reshape(orbitals, width)
    term[...] = total
    for order in range(1, TERMS):
        term_high, term_low = split(term[...])
        pair = jnp.concatenate([term_high, term_low], axis=1)
        both = dot(high[...], pair)
        value = both[:, :width] + both[:, width:] + dot(low[...], term_high)
        value = value.reshape(-1, own, SUBLANES, width)
        placed = jnp.zeros((value.shape[0], SUBLANES, width), F32)
        for j in range(own):
            for s in range(own):
                shift = ((j - s) * unit) % SUBLANES
                moved = pltpu.roll(value[:, j], shift, 1) if shift else value[:, j]
                placed = jnp.where((sub == j) & (lane == s), moved, placed)
        placed = placed.reshape(orbitals, width) / order
        term[...] = placed
        total = total + placed
    flipped = total.T
    for s in range(own):
        out[s] = flipped[s * occupied : (s + 1) * occupied, :]


def taylor(tiles, base, own, orbitals, occupied):
    width = own * occupied
    chunks = len(tiles)
    devices = tiles[0].shape[0]
    half = orbitals // devices // 2
    begin = []
    if half % SUBLANES or own != 2:
        start = tiles[0][:, base : base + own * half].reshape(devices, own, half, 2, occupied)
        begin = [start.transpose(0, 3, 2, 1, 4).reshape(orbitals, width)]
    vmem = pl.BlockSpec(memory_space=pltpu.VMEM)
    return pl.pallas_call(
        functools.partial(taylor_kernel, own, chunks, base),
        out_shape=jax.ShapeDtypeStruct((own, occupied, orbitals), F32),
        in_specs=[vmem] * (chunks + len(begin)),
        out_specs=vmem,
        scratch_shapes=[
            pltpu.VMEM((own * orbitals, orbitals), BF16),
            pltpu.VMEM((own * orbitals, orbitals), BF16),
            pltpu.VMEM((orbitals, width), F32),
        ],
        compiler_params=params(24),
    )(*tiles, *begin)


def per_device(trial, walkers, chol, field_noise, log_weight, parent):
    own, orbitals, occupied = walkers.shape
    walk_size = lax.axis_size("walk")
    chol_size = lax.axis_size("chol")
    devices = walk_size * chol_size
    vectors, pairs = chol.shape
    rows_here = pairs // orbitals
    half = rows_here // 2
    place = lax.axis_index(BOTH)

    sent, pair, begun = rotate(devices, parent, trial.T, walkers.transpose(0, 2, 1), chol)
    rotated = lax.all_to_all(sent, BOTH, split_axis=0, concat_axis=0, tiled=True)
    contracted = contract(pair, chol, begun)
    mine = partial_fields(own, half, place.reshape(1), rotated, contracted, field_noise)
    fields = sum_everywhere(mine, walk_size, chol_size)

    parents = rotated[:, 2 * own * half, :own].T.reshape(own * devices).astype(jnp.int32)
    orbital_rows = carry(own, half, (parents % own) * devices + parents // own, rotated)
    scaled = select(row_of(parents, own, walk_size, chol_size), fields)
    places = row_of(place * own + jnp.arange(own, dtype=jnp.int32), own, walk_size, chol_size)

    unit = SUBLANES // own
    units = rows_here // unit
    cuts = [0] + ([FIRST_UNITS] if units > FIRST_UNITS else []) + [units]
    tiles = []
    for begin, end in zip(cuts[:-1], cuts[1:]):
        along = () if begin else (orbital_rows, fields, field_noise, places, log_weight)
        chunk = potential_tiles(own, scaled, chol, orbitals, begin * unit, (end - begin) * unit, along)
        chunk = chunk.reshape(devices, -1, LANES)
        tiles.append(lax.all_to_all(chunk, BOTH, split_axis=0, concat_axis=0, tiled=True))

    base = own * cuts[1] * unit * orbitals // LANES
    new_walkers = taylor(tiles, base, own, orbitals, occupied).transpose(0, 2, 1)
    new_log_weight = tiles[0][parent // own, base + own * half, parent % own]
    return (new_walkers, new_log_weight)


def solution(mesh):
    return jax.shard_map(
        per_device,
        mesh=mesh,
        in_specs=(
            P(),
            P(BOTH, None, None),
            P(None, BOTH),
            P(BOTH, None),
            P(BOTH),
            P(BOTH),
        ),
        out_specs=(P(BOTH, None, None), P(BOTH)),
        check_vma=False,
    )
```

```python
import functools

import jax
import jax.numpy as jnp
from jax import lax
from jax.experimental import pallas as pl
from jax.experimental.pallas import tpu as pltpu
from jax.sharding import PartitionSpec as P

TERMS = 6
PRECISE = lax.Precision.HIGHEST
TIME_ROOT = 0.1
BOTH = ("walk", "chol")
LANES = 128
SUBLANES = 8
F32 = jnp.float32
BF16 = jnp.bfloat16
MIB = 1024 * 1024
FIRST_UNITS = 1
HEAD = 768
PIECE = 128


def params(mib):
    return pltpu.CompilerParams(vmem_limit_bytes=mib * MIB)


def whole(shape):
    zeros = (0,) * len(shape)
    return pl.BlockSpec(shape, lambda *_: zeros)


def dot(a, b):
    return jnp.dot(a, b, preferred_element_type=F32)


def dot_nt(a, b):
    return lax.dot_general(a, b, (((1,), (1,)), ((), ())), preferred_element_type=F32)


def split(x):
    high = x.astype(BF16)
    low = (x - high.astype(F32)).astype(BF16)
    return high, low


def rotate_kernel(devices, parent, trial_in, walkers_in, chol, sent, pair, contracted, trial, walkers, loaded, done, sems):
    own, occupied, orbitals = walkers.shape
    half = orbitals // devices // 2
    count = loaded.shape[0] // PIECE
    small = [
        pltpu.make_async_copy(walkers_in, walkers, sems.at[0]),
        pltpu.make_async_copy(trial_in, trial, sems.at[1]),
    ]
    reads, writes = [], []
    for p in range(count):
        at = pl.ds(p * PIECE, PIECE)
        reads.append(pltpu.make_async_copy(chol.at[at], loaded.at[at], sems.at[2 + p]))
        writes.append(pltpu.make_async_copy(done.at[at], contracted.at[at], sems.at[2 + count + p]))
    for copy in small + reads:
        copy.start()
    for copy in small:
        copy.wait()
    lane = jax.lax.broadcasted_iota(jnp.int32, (1, LANES), 1)
    both_parts = jnp.concatenate([trial[...]] * 2, axis=0).T
    high, low = split(both_parts)
    both_parts = jnp.where(lane < occupied, high, low)
    pair[...] = both_parts
    alone = jnp.where(lane < occupied, both_parts, jnp.zeros_like(both_parts))
    rows = jax.lax.broadcasted_iota(jnp.int32, (occupied, 1), 0)
    state = []
    for s in range(own):
        crossed = lax.dot_general(
            walkers[s], trial[...], (((1,), (1,)), ((), ())), precision=PRECISE, preferred_element_type=F32
        )
        normal = lax.dot_general(
            crossed, crossed, (((1,), (1,)), ((), ())), precision=PRECISE, preferred_element_type=F32
        )
        state.append(jnp.concatenate([normal, crossed], axis=1))

    def eliminate(k):
        for s in range(own):
            m = state[s]
            pivot = m[k : k + 1, :]
            scaled = pivot / m[k : k + 1, k : k + 1]
            state[s] = jnp.where(rows == k, scaled, m - m[:, k : k + 1] * scaled)

    pivots = 0
    for p in range(count):
        reads[p].wait()
        at = slice(p * PIECE, (p + 1) * PIECE)
        for i in range(half):
            ends = [contract_row(loaded[at, r * orbitals : (r + 1) * orbitals], both_parts, alone) for r in (i, i + half)]
            done[at, i * LANES : (i + 1) * LANES] = jnp.where(lane < occupied, ends[0], ends[1])
            upto = occupied * (p * half + i + 1) // (count * half)
            for k in range(pivots, upto):
                eliminate(k)
            pivots = upto
        writes[p].start()
    packed = jnp.concatenate([walkers[s] for s in range(own)], axis=0).T
    empty = jnp.zeros((occupied, occupied), F32)
    inverse = jnp.concatenate(
        [
            jnp.concatenate([state[s][:, occupied:] if s == c else empty for c in range(own)], axis=1)
            for s in range(own)
        ],
        axis=0,
    )
    rotated = jnp.dot(packed, inverse, precision=PRECISE, preferred_element_type=F32)
    for at, value in ((0, rotated), (own * half, packed)):
        blocks = value.reshape(devices, 2, half, LANES)
        first, second = blocks[:, 0], blocks[:, 1]
        sent[:, at : at + half, :] = jnp.where(lane < occupied, first, pltpu.roll(second, occupied, 2))
        sent[:, at + half : at + 2 * half, :] = jnp.where(lane < occupied, pltpu.roll(first, occupied, 2), second)
    extra = jnp.zeros((SUBLANES, LANES), F32)
    for s in range(own):
        extra = jnp.where(lane == s, parent[s].astype(F32), extra)
    tail = sent.shape[1] - 2 * own * half
    sent[:, 2 * own * half :, :] = jnp.broadcast_to(extra[None, :tail], (devices, tail, LANES))
    for copy in writes:
        copy.wait()


def rotate_plain(devices, parent, trial, walkers, sent_rows):
    own, occupied, orbitals = walkers.shape
    half = orbitals // devices // 2
    crossed = jnp.einsum("wkm,nm->wkn", walkers, trial, precision=PRECISE)
    normal = jnp.einsum("wkn,wln->wkl", crossed, crossed, precision=PRECISE)
    factor = jnp.linalg.cholesky(normal)
    inverse = jax.vmap(lambda f, c: jax.scipy.linalg.cho_solve((f, True), c))(factor, crossed)
    rotated = jnp.einsum("wkm,wkn->wmn", walkers, inverse, precision=PRECISE)
    sent = jnp.concatenate([rotated, walkers.transpose(0, 2, 1)], axis=0)
    sent = sent.reshape(2 * own, devices, 2, half, occupied).transpose(1, 0, 3, 2, 4)
    sent = sent.reshape(devices, 2 * own * half, 2 * occupied)
    extra = jnp.zeros((sent_rows - 2 * own * half, LANES), F32).at[0, :own].set(parent.astype(F32))
    sent = jnp.concatenate([sent, jnp.broadcast_to(extra[None], (devices,) + extra.shape)], axis=1)
    return sent, jnp.concatenate(split(trial.T), axis=1)


def eights(rows):
    return -(-rows // SUBLANES) * SUBLANES


def rotate(devices, parent, trial, walkers, chol):
    own, occupied, orbitals = walkers.shape
    vectors = chol.shape[0]
    columns = chol.shape[1] // orbitals * occupied
    half = orbitals // devices // 2
    sent_rows = eights(2 * own * half + 1)
    if half % SUBLANES or own != 2 or own * occupied != LANES:
        return rotate_plain(devices, parent, trial, walkers, sent_rows) + (None,)
    anywhere = pl.BlockSpec(memory_space=pl.ANY)
    return pl.pallas_call(
        functools.partial(rotate_kernel, devices),
        grid=(1,),
        out_shape=(
            jax.ShapeDtypeStruct((devices, sent_rows, LANES), F32),
            jax.ShapeDtypeStruct((orbitals, 2 * occupied), BF16),
            jax.ShapeDtypeStruct((vectors, columns), F32),
        ),
        in_specs=[pl.BlockSpec(memory_space=pltpu.SMEM), anywhere, anywhere, anywhere],
        out_specs=(whole((devices, sent_rows, LANES)), whole((orbitals, 2 * occupied)), anywhere),
        scratch_shapes=[
            pltpu.VMEM(trial.shape, F32),
            pltpu.VMEM(walkers.shape, F32),
            pltpu.VMEM((HEAD, chol.shape[1]), F32),
            pltpu.VMEM((HEAD, columns), F32),
            pltpu.SemaphoreType.DMA((2 + 2 * (HEAD // PIECE),)),
        ],
        compiler_params=params(60),
    )(parent, trial, walkers, chol)


def contract_row(part, both_parts, alone):
    chol_high, chol_low = split(part)
    both = dot(chol_high, both_parts) + dot(chol_low, alone)
    return both + pltpu.roll(both, both.shape[1] // 2, 1)


def contract_kernel(pair, chol, *refs):
    out = refs[-1]
    orbitals = pair.shape[0]
    occupied = pair.shape[1] // 2
    half = chol.shape[1] // orbitals // 2
    lane = jax.lax.broadcasted_iota(jnp.int32, (1, 2 * occupied), 1)
    both_parts = pair[...]
    alone = jnp.where(lane < occupied, both_parts, jnp.zeros_like(both_parts))
    for i in range(half):
        ends = [contract_row(chol[:, r * orbitals : (r + 1) * orbitals], both_parts, alone) for r in (i, i + half)]
        out[:, i * 2 * occupied : (i + 1) * 2 * occupied] = jnp.where(lane < occupied, ends[0], ends[1])


def contract(pair, chol, begun):
    vectors, pairs = chol.shape
    orbitals, occupied = pair.shape[0], pair.shape[1] // 2
    columns = pairs // orbitals * occupied
    block = 256
    skip = 0 if begun is None else HEAD // block
    more = [] if begun is None else [begun]
    rest = vectors - skip * block
    return pl.pallas_call(
        contract_kernel,
        grid=(rest // block,),
        out_shape=jax.ShapeDtypeStruct((vectors, columns), F32),
        in_specs=[whole(pair.shape), pl.BlockSpec((block, pairs), lambda g: (g + skip, 0))]
        + [pl.BlockSpec(memory_space=pl.ANY)] * len(more),
        out_specs=pl.BlockSpec((block, columns), lambda g: (g + skip, 0)),
        input_output_aliases={2: 0} if more else {},
        compiler_params=params(60),
        cost_estimate=pl.CostEstimate(
            flops=2 * rest * pairs * occupied * 3, bytes_accessed=4 * rest * (pairs + columns), transcendentals=0
        ),
    )(pair, chol, *more)


def bias_kernel(own, half, place, rotated, noise, contracted, out, stacked, loaded, sems):
    devices = rotated.shape[0]
    slots = own * devices
    count = sems.shape[0]
    block = loaded.shape[0] // count
    copies = []
    for g in range(count):
        at = pl.ds(g * block, block)
        copies.append(pltpu.make_async_copy(contracted.at[at], loaded.at[at], sems.at[g]))
    for copy in copies:
        copy.start()
    for i in range(half):
        for s in range(own):
            high, low = split(rotated[:, s * half + i, :])
            at = s * devices
            stacked[at : at + devices, i * LANES : (i + 1) * LANES] = high
            stacked[slots + at : slots + at + devices, i * LANES : (i + 1) * LANES] = low
    rows = jax.lax.broadcasted_iota(jnp.int32, (slots, 1), 0)

    def step(g, carry):
        at = pl.ds(pl.multiple_of(g * block, LANES), block)
        pltpu.make_async_copy(contracted.at[at], loaded.at[at], sems.at[g]).wait()
        b_high, b_low = split(loaded[at, :])
        both = dot_nt(stacked[...], b_high) + dot_nt(stacked[...], b_low)
        value = -TIME_ROOT * (both[:slots] + both[slots:])
        for s in range(own):
            value += jnp.where(rows == s * devices + place[0], noise[s : s + 1, at], 0.0)
        out[:, at] = value
        return carry

    lax.fori_loop(0, count, step, 0)


def partial_fields(own, half, place, rotated, contracted, noise):
    vectors, columns = contracted.shape
    devices = rotated.shape[0]
    count = vectors // 512
    return pl.pallas_call(
        functools.partial(bias_kernel, own, half),
        grid=(1,),
        out_shape=jax.ShapeDtypeStruct((own * devices, vectors), F32),
        in_specs=[
            pl.BlockSpec(memory_space=pltpu.SMEM),
            whole(rotated.shape),
            whole(noise.shape),
            pl.BlockSpec(memory_space=pl.ANY),
        ],
        out_specs=whole((own * devices, vectors)),
        scratch_shapes=[
            pltpu.VMEM((2 * own * devices, columns), BF16),
            pltpu.VMEM(contracted.shape, F32),
            pltpu.SemaphoreType.DMA((count,)),
        ],
        compiler_params=params(52),
    )(place, rotated, noise, contracted)


def send(x, walk_size, chol_size, target):
    return lax.ppermute(x, BOTH, [(i, target(i)) for i in range(walk_size * chol_size)])


def sum_everywhere(x, walk_size, chol_size):
    walk = lax.axis_index("walk")
    core = lax.axis_index("chol") % 2
    half = x.shape[0] // 2
    quarter = half // walk_size
    mine = lax.dynamic_slice_in_dim(x, core * half, half, 0)
    other = lax.dynamic_slice_in_dim(x, (1 - core) * half, half, 0)
    chip = mine + send(other, walk_size, chol_size, lambda i: i ^ 1)
    total = lax.dynamic_slice_in_dim(chip, walk * quarter, quarter, 0)
    got = [
        send(
            lax.dynamic_slice_in_dim(chip, (walk ^ r) * quarter, quarter, 0),
            walk_size, chol_size, lambda i, r=r: i ^ (r * chol_size),
        )
        for r in range(1, walk_size)
    ]
    for g in got:
        total = total + g
    got = [send(total, walk_size, chol_size, lambda i, r=r: i ^ (2 * r)) for r in range(1, chol_size // 2)]
    for g in got:
        total = total + g
    blocks = [total] + [
        send(total, walk_size, chol_size, lambda i, r=r: i ^ (r * chol_size)) for r in range(1, walk_size)
    ]
    here = jnp.concatenate(blocks, axis=0)
    there = send(here, walk_size, chol_size, lambda i: i ^ 1)
    return jnp.concatenate([here, there], axis=0)


def row_of(walker, own, walk_size, chol_size):
    everyone = own * walk_size * chol_size
    walk = lax.axis_index("walk")
    core = lax.axis_index("chol") % 2
    row = (walker % own) * (walk_size * chol_size) + walker // own
    half = everyone // 2
    quarter = half // walk_size
    inside = row % half
    return ((row // half) ^ core) * half + ((inside // quarter) ^ walk) * quarter + inside % quarter


def select_kernel(rows, fields, out):
    slots = fields.shape[0]
    lane = jax.lax.broadcasted_iota(jnp.int32, (slots, slots), 1)
    pick = jnp.where(lane == rows[...], 1.0, 0.0).astype(BF16)
    value = fields[...]
    first, rest = split(value)
    second, third = split(value - first.astype(F32))
    picked = dot(pick, first) + dot(pick, second) + dot(pick, third)
    high, low = split(TIME_ROOT * picked)
    out[:slots, :] = high
    out[slots:, :] = low


def select(rows, fields):
    slots, vectors = fields.shape
    block = 512
    return pl.pallas_call(
        select_kernel,
        grid=(vectors // block,),
        out_shape=jax.ShapeDtypeStruct((2 * slots, vectors), BF16),
        in_specs=[whole((slots, 1)), pl.BlockSpec((slots, block), lambda g: (0, g))],
        out_specs=pl.BlockSpec((2 * slots, block), lambda g: (0, g)),
        compiler_params=params(16),
    )(rows.reshape(slots, 1), fields)


def carry_kernel(own, half, rows, received, out):
    devices = received.shape[0]
    slots = own * devices
    lane = jax.lax.broadcasted_iota(jnp.int32, (slots, slots), 1)
    pick = jnp.where(lane == rows[...], 1.0, 0.0).astype(BF16)
    for i in range(half):
        value = jnp.concatenate([received[:, (own + s) * half + i, :] for s in range(own)], axis=0)
        first, rest = split(value)
        second, third = split(value - first.astype(F32))
        picked = dot(pick, first) + dot(pick, second) + dot(pick, third)
        for s in range(own):
            out[s * half + i] = picked[s * devices : (s + 1) * devices]


def carry(own, half, rows, received):
    devices = received.shape[0]
    shape = (own * half, devices, LANES)
    return pl.pallas_call(
        functools.partial(carry_kernel, own, half),
        grid=(1,),
        out_shape=jax.ShapeDtypeStruct(shape, F32),
        in_specs=[whole((own * devices, 1)), whole(received.shape)],
        out_specs=whole(shape),
        compiler_params=params(16),
    )(rows.reshape(-1, 1), received)


def potential_kernel(own, parts, base, fields, *refs):
    chols, out = refs[:parts], refs[-1]
    slots = fields.shape[0] // 2
    devices = slots // own
    unit = SUBLANES // own
    step = chols[0].shape[0]
    pieces = chols[0].shape[1] // LANES
    total = None
    for p in range(parts):
        high, low = split(chols[p][...])
        part = fields[:, p * step : (p + 1) * step]
        value = dot(part, high) + dot(part, low)
        total = value if total is None else total + value
    total = total[:slots] + total[slots:]
    here = pl.program_id(0)
    start = here // unit * (pieces * SUBLANES) + here % unit
    stride = out.shape[0] // devices
    for t in range(pieces):
        for s in range(own):
            at = pl.ds(start + t * SUBLANES + s * unit, devices, stride=stride)
            out[at, :] = total[s * devices : (s + 1) * devices, t * LANES : (t + 1) * LANES]
    if len(refs) == parts + 1:
        return
    orbital_rows, summed, noise, places, levels = refs[parts:-1]

    @pl.when(here == 0)
    def _():
        lane = jax.lax.broadcasted_iota(jnp.int32, (1, LANES), 1)
        line = jnp.zeros((1, LANES), F32)
        for s in range(own):
            shift = noise[s : s + 1, :] - summed[pl.ds(places[s], 1), :]
            terms = 0.5 * shift * shift - noise[s : s + 1, :] * shift
            line = jnp.where(lane == s, levels[s] + jnp.sum(terms, axis=1, keepdims=True), line)
        taken = orbital_rows.shape[0]
        for r in range(taken):
            out[pl.ds(base + r, devices, stride=stride), :] = orbital_rows[r]
        for r in range(taken, stride - base):
            out[pl.ds(base + r, devices, stride=stride), :] = jnp.broadcast_to(line, (devices, LANES))


def potential_tiles(own, fields, chol, orbitals, first, count, along):
    vectors = chol.shape[0]
    slots = fields.shape[0] // 2
    step = 256
    parts = vectors // step
    devices = slots // own
    base = own * count * orbitals // LANES
    rows = devices * base
    smem = pl.BlockSpec(memory_space=pltpu.SMEM)
    more = []
    if along:
        rows += devices * eights(along[0].shape[0] + 1)
        more = [whole(a.shape) for a in along[:3]] + [smem, smem]
    return pl.pallas_call(
        functools.partial(potential_kernel, own, parts, base),
        grid=(count,),
        out_shape=jax.ShapeDtypeStruct((rows, LANES), F32),
        in_specs=[whole(fields.shape)]
        + [pl.BlockSpec((step, orbitals), lambda i, p=p: (p, first + i)) for p in range(parts)]
        + more,
        out_specs=whole((rows, LANES)),
        compiler_params=params(32),
        cost_estimate=pl.CostEstimate(
            flops=2 * slots * vectors * orbitals * count * 3,
            bytes_accessed=4 * vectors * orbitals * count,
            transcendentals=0,
        ),
    )(fields, *[chol] * parts, *along)


def taylor_kernel(own, chunks, base, *refs):
    tiles = refs[:chunks]
    begin = refs[chunks:-4]
    out, high, low, term = refs[-4:]
    orbitals, width = term.shape
    occupied = width // own
    pieces = orbitals // LANES
    devices = tiles[0].shape[0]
    half = orbitals // devices // 2
    unit = SUBLANES // own
    lane = jax.lax.broadcasted_iota(jnp.int32, (1, width), 1) // occupied
    sub = jax.lax.broadcasted_iota(jnp.int32, (SUBLANES, 1), 0) // unit
    for t in range(pieces):
        parts = []
        for c, tile in enumerate(tiles):
            value = tile[:, :base, :] if c == 0 else tile[...]
            parts.append(value.reshape(devices, -1, pieces, SUBLANES, LANES)[:, :, t])
        value_high, value_low = split(jnp.concatenate(parts, axis=1).reshape(-1, LANES))
        high[:, t * LANES : (t + 1) * LANES] = value_high
        low[:, t * LANES : (t + 1) * LANES] = value_low
    if begin:
        total = begin[0][...]
    else:
        left = tiles[0][:, base : base + half, :]
        right = tiles[0][:, base + half : base + 2 * half, :]
        upper = jnp.where(lane == 0, left, pltpu.roll(right, occupied, 2))
        lower = jnp.where(lane == 0, pltpu.roll(left, occupied, 2), right)
        total = jnp.stack([upper, lower], axis=1).reshape(orbitals, width)
    term[...] = total
    for order in range(1, TERMS):
        term_high, term_low = split(term[...])
        pair = jnp.concatenate([term_high, term_low], axis=1)
        both = dot(high[...], pair)
        value = both[:, :width] + both[:, width:] + dot(low[...], term_high)
        value = value.reshape(-1, own, SUBLANES, width)
        placed = jnp.zeros((value.shape[0], SUBLANES, width), F32)
        for j in range(own):
            for s in range(own):
                shift = ((j - s) * unit) % SUBLANES
                moved = pltpu.roll(value[:, j], shift, 1) if shift else value[:, j]
                placed = jnp.where((sub == j) & (lane == s), moved, placed)
        placed = placed.reshape(orbitals, width) / order
        term[...] = placed
        total = total + placed
    flipped = total.T
    for s in range(own):
        out[s] = flipped[s * occupied : (s + 1) * occupied, :]


def taylor(tiles, base, own, orbitals, occupied):
    width = own * occupied
    chunks = len(tiles)
    devices = tiles[0].shape[0]
    half = orbitals // devices // 2
    begin = []
    if half % SUBLANES or own != 2:
        start = tiles[0][:, base : base + own * half].reshape(devices, own, half, 2, occupied)
        begin = [start.transpose(0, 3, 2, 1, 4).reshape(orbitals, width)]
    vmem = pl.BlockSpec(memory_space=pltpu.VMEM)
    return pl.pallas_call(
        functools.partial(taylor_kernel, own, chunks, base),
        out_shape=jax.ShapeDtypeStruct((own, occupied, orbitals), F32),
        in_specs=[vmem] * (chunks + len(begin)),
        out_specs=vmem,
        scratch_shapes=[
            pltpu.VMEM((own * orbitals, orbitals), BF16),
            pltpu.VMEM((own * orbitals, orbitals), BF16),
            pltpu.VMEM((orbitals, width), F32),
        ],
        compiler_params=params(24),
    )(*tiles, *begin)


def per_device(trial, walkers, chol, field_noise, log_weight, parent):
    own, orbitals, occupied = walkers.shape
    walk_size = lax.axis_size("walk")
    chol_size = lax.axis_size("chol")
    devices = walk_size * chol_size
    vectors, pairs = chol.shape
    rows_here = pairs // orbitals
    half = rows_here // 2
    place = lax.axis_index(BOTH)

    sent, pair, begun = rotate(devices, parent, trial.T, walkers.transpose(0, 2, 1), chol)
    rotated = lax.all_to_all(sent, BOTH, split_axis=0, concat_axis=0, tiled=True)
    contracted = contract(pair, chol, begun)
    mine = partial_fields(own, half, place.reshape(1), rotated, contracted, field_noise)
    fields = sum_everywhere(mine, walk_size, chol_size)

    parents = rotated[:, 2 * own * half, :own].T.reshape(own * devices).astype(jnp.int32)
    orbital_rows = carry(own, half, (parents % own) * devices + parents // own, rotated)
    scaled = select(row_of(parents, own, walk_size, chol_size), fields)
    places = row_of(place * own + jnp.arange(own, dtype=jnp.int32), own, walk_size, chol_size)

    unit = SUBLANES // own
    units = rows_here // unit
    cuts = [0] + ([FIRST_UNITS] if units > FIRST_UNITS else []) + [units]
    tiles = []
    for begin, end in zip(cuts[:-1], cuts[1:]):
        along = () if begin else (orbital_rows, fields, field_noise, places, log_weight)
        chunk = potential_tiles(own, scaled, chol, orbitals, begin * unit, (end - begin) * unit, along)
        chunk = chunk.reshape(devices, -1, LANES)
        tiles.append(lax.all_to_all(chunk, BOTH, split_axis=0, concat_axis=0, tiled=True))

    base = own * cuts[1] * unit * orbitals // LANES
    new_walkers = taylor(tiles, base, own, orbitals, occupied).transpose(0, 2, 1)
    new_log_weight = tiles[0][parent // own, base + own * half, parent % own]
    return (new_walkers, new_log_weight)


def solution(mesh):
    return jax.shard_map(
        per_device,
        mesh=mesh,
        in_specs=(
            P(),
            P(BOTH, None, None),
            P(None, BOTH),
            P(BOTH, None),
            P(BOTH),
            P(BOTH),
        ),
        out_specs=(P(BOTH, None, None), P(BOTH)),
        check_vma=False,
    )
```

```python
import functools

import jax
import jax.numpy as jnp
from jax import lax
from jax.experimental import pallas as pl
from jax.experimental.pallas import tpu as pltpu
from jax.sharding import PartitionSpec as P

TERMS = 6
PRECISE = lax.Precision.HIGHEST
TIME_ROOT = 0.1
BOTH = ("walk", "chol")
LANES = 128
SUBLANES = 8
F32 = jnp.float32
BF16 = jnp.bfloat16
MIB = 1024 * 1024
FIRST_UNITS = 1
HEAD = 768
PIECE = 128


def params(mib):
    return pltpu.CompilerParams(vmem_limit_bytes=mib * MIB)


def whole(shape):
    zeros = (0,) * len(shape)
    return pl.BlockSpec(shape, lambda *_: zeros)


def dot(a, b):
    return jnp.dot(a, b, preferred_element_type=F32)


def dot_nt(a, b):
    return lax.dot_general(a, b, (((1,), (1,)), ((), ())), preferred_element_type=F32)


def split(x):
    high = x.astype(BF16)
    low = (x - high.astype(F32)).astype(BF16)
    return high, low


def rotate_kernel(devices, parent, trial_in, walkers_in, chol, sent, pair, contracted, trial, walkers, loaded, done, sems):
    own, occupied, orbitals = walkers.shape
    half = orbitals // devices // 2
    count = loaded.shape[0] // PIECE
    small = [
        pltpu.make_async_copy(walkers_in, walkers, sems.at[0]),
        pltpu.make_async_copy(trial_in, trial, sems.at[1]),
    ]
    reads, writes = [], []
    for p in range(count):
        at = pl.ds(p * PIECE, PIECE)
        reads.append(pltpu.make_async_copy(chol.at[at], loaded.at[at], sems.at[2 + p]))
        writes.append(pltpu.make_async_copy(done.at[at], contracted.at[at], sems.at[2 + count + p]))
    for copy in small + reads:
        copy.start()
    for copy in small:
        copy.wait()
    lane = jax.lax.broadcasted_iota(jnp.int32, (1, LANES), 1)
    both_parts = jnp.concatenate([trial[...]] * 2, axis=0).T
    high, low = split(both_parts)
    both_parts = jnp.where(lane < occupied, high, low)
    pair[...] = both_parts
    alone = jnp.where(lane < occupied, both_parts, jnp.zeros_like(both_parts))
    rows = jax.lax.broadcasted_iota(jnp.int32, (occupied, 1), 0)
    state = []
    for s in range(own):
        crossed = lax.dot_general(
            walkers[s], trial[...], (((1,), (1,)), ((), ())), precision=PRECISE, preferred_element_type=F32
        )
        normal = lax.dot_general(
            crossed, crossed, (((1,), (1,)), ((), ())), precision=PRECISE, preferred_element_type=F32
        )
        state.append(jnp.concatenate([normal, crossed], axis=1))

    def eliminate(k):
        for s in range(own):
            m = state[s]
            pivot = m[k : k + 1, :]
            scaled = pivot / m[k : k + 1, k : k + 1]
            state[s] = jnp.where(rows == k, scaled, m - m[:, k : k + 1] * scaled)

    pivots = 0
    for p in range(count):
        reads[p].wait()
        at = slice(p * PIECE, (p + 1) * PIECE)
        for i in range(half):
            ends = [contract_row(loaded[at, r * orbitals : (r + 1) * orbitals], both_parts, alone) for r in (i, i + half)]
            done[at, i * LANES : (i + 1) * LANES] = jnp.where(lane < occupied, ends[0], ends[1])
            upto = occupied * (p * half + i + 1) // (count * half)
            for k in range(pivots, upto):
                eliminate(k)
            pivots = upto
        writes[p].start()
    packed = jnp.concatenate([walkers[s] for s in range(own)], axis=0).T
    empty = jnp.zeros((occupied, occupied), F32)
    inverse = jnp.concatenate(
        [
            jnp.concatenate([state[s][:, occupied:] if s == c else empty for c in range(own)], axis=1)
            for s in range(own)
        ],
        axis=0,
    )
    rotated = jnp.dot(packed, inverse, precision=PRECISE, preferred_element_type=F32)
    for at, value in ((0, rotated), (own * half, packed)):
        blocks = value.reshape(devices, 2, half, LANES)
        first, second = blocks[:, 0], blocks[:, 1]
        sent[:, at : at + half, :] = jnp.where(lane < occupied, first, pltpu.roll(second, occupied, 2))
        sent[:, at + half : at + 2 * half, :] = jnp.where(lane < occupied, pltpu.roll(first, occupied, 2), second)
    extra = jnp.zeros((SUBLANES, LANES), F32)
    for s in range(own):
        extra = jnp.where(lane == s, parent[s].astype(F32), extra)
    tail = sent.shape[1] - 2 * own * half
    sent[:, 2 * own * half :, :] = jnp.broadcast_to(extra[None, :tail], (devices, tail, LANES))
    for copy in writes:
        copy.wait()


def rotate_plain(devices, parent, trial, walkers, sent_rows):
    own, occupied, orbitals = walkers.shape
    half = orbitals // devices // 2
    crossed = jnp.einsum("wkm,nm->wkn", walkers, trial, precision=PRECISE)
    normal = jnp.einsum("wkn,wln->wkl", crossed, crossed, precision=PRECISE)
    factor = jnp.linalg.cholesky(normal)
    inverse = jax.vmap(lambda f, c: jax.scipy.linalg.cho_solve((f, True), c))(factor, crossed)
    rotated = jnp.einsum("wkm,wkn->wmn", walkers, inverse, precision=PRECISE)
    sent = jnp.concatenate([rotated, walkers.transpose(0, 2, 1)], axis=0)
    sent = sent.reshape(2 * own, devices, 2, half, occupied).transpose(1, 0, 3, 2, 4)
    sent = sent.reshape(devices, 2 * own * half, 2 * occupied)
    extra = jnp.zeros((sent_rows - 2 * own * half, LANES), F32).at[0, :own].set(parent.astype(F32))
    sent = jnp.concatenate([sent, jnp.broadcast_to(extra[None], (devices,) + extra.shape)], axis=1)
    return sent, jnp.concatenate(split(trial.T), axis=1)


def eights(rows):
    return -(-rows // SUBLANES) * SUBLANES


def rotate(devices, parent, trial, walkers, chol):
    own, occupied, orbitals = walkers.shape
    vectors = chol.shape[0]
    columns = chol.shape[1] // orbitals * occupied
    half = orbitals // devices // 2
    sent_rows = eights(2 * own * half + 1)
    if half % SUBLANES or own != 2 or own * occupied != LANES:
        return rotate_plain(devices, parent, trial, walkers, sent_rows) + (None,)
    anywhere = pl.BlockSpec(memory_space=pl.ANY)
    return pl.pallas_call(
        functools.partial(rotate_kernel, devices),
        grid=(1,),
        out_shape=(
            jax.ShapeDtypeStruct((devices, sent_rows, LANES), F32),
            jax.ShapeDtypeStruct((orbitals, 2 * occupied), BF16),
            jax.ShapeDtypeStruct((vectors, columns), F32),
        ),
        in_specs=[pl.BlockSpec(memory_space=pltpu.SMEM), anywhere, anywhere, anywhere],
        out_specs=(whole((devices, sent_rows, LANES)), whole((orbitals, 2 * occupied)), anywhere),
        scratch_shapes=[
            pltpu.VMEM(trial.shape, F32),
            pltpu.VMEM(walkers.shape, F32),
            pltpu.VMEM((HEAD, chol.shape[1]), F32),
            pltpu.VMEM((HEAD, columns), F32),
            pltpu.SemaphoreType.DMA((2 + 2 * (HEAD // PIECE),)),
        ],
        compiler_params=params(60),
    )(parent, trial, walkers, chol)


def contract_row(part, both_parts, alone):
    chol_high, chol_low = split(part)
    both = dot(chol_high, both_parts) + dot(chol_low, alone)
    return both + pltpu.roll(both, both.shape[1] // 2, 1)


def contract_kernel(pair, chol, *refs):
    out = refs[-1]
    orbitals = pair.shape[0]
    occupied = pair.shape[1] // 2
    half = chol.shape[1] // orbitals // 2
    lane = jax.lax.broadcasted_iota(jnp.int32, (1, 2 * occupied), 1)
    both_parts = pair[...]
    alone = jnp.where(lane < occupied, both_parts, jnp.zeros_like(both_parts))
    for i in range(half):
        ends = [contract_row(chol[:, r * orbitals : (r + 1) * orbitals], both_parts, alone) for r in (i, i + half)]
        out[:, i * 2 * occupied : (i + 1) * 2 * occupied] = jnp.where(lane < occupied, ends[0], ends[1])


def contract(pair, chol, begun):
    vectors, pairs = chol.shape
    orbitals, occupied = pair.shape[0], pair.shape[1] // 2
    columns = pairs // orbitals * occupied
    block = 256
    skip = 0 if begun is None else HEAD // block
    more = [] if begun is None else [begun]
    rest = vectors - skip * block
    return pl.pallas_call(
        contract_kernel,
        grid=(rest // block,),
        out_shape=jax.ShapeDtypeStruct((vectors, columns), F32),
        in_specs=[whole(pair.shape), pl.BlockSpec((block, pairs), lambda g: (g + skip, 0))]
        + [pl.BlockSpec(memory_space=pl.ANY)] * len(more),
        out_specs=pl.BlockSpec((block, columns), lambda g: (g + skip, 0)),
        input_output_aliases={2: 0} if more else {},
        compiler_params=params(60),
        cost_estimate=pl.CostEstimate(
            flops=2 * rest * pairs * occupied * 3, bytes_accessed=4 * rest * (pairs + columns), transcendentals=0
        ),
    )(pair, chol, *more)


def bias_kernel(own, half, place, rotated, noise, contracted, out, stacked, loaded, sems):
    devices = rotated.shape[0]
    slots = own * devices
    count = sems.shape[0]
    block = loaded.shape[0] // count
    copies = []
    for g in range(count):
        at = pl.ds(g * block, block)
        copies.append(pltpu.make_async_copy(contracted.at[at], loaded.at[at], sems.at[g]))
    for copy in copies:
        copy.start()
    for i in range(half):
        for s in range(own):
            high, low = split(rotated[:, s * half + i, :])
            at = s * devices
            stacked[at : at + devices, i * LANES : (i + 1) * LANES] = high
            stacked[slots + at : slots + at + devices, i * LANES : (i + 1) * LANES] = low
    rows = jax.lax.broadcasted_iota(jnp.int32, (slots, 1), 0)

    def step(g, carry):
        at = pl.ds(pl.multiple_of(g * block, LANES), block)
        pltpu.make_async_copy(contracted.at[at], loaded.at[at], sems.at[g]).wait()
        b_high, b_low = split(loaded[at, :])
        both = dot_nt(stacked[...], b_high) + dot_nt(stacked[...], b_low)
        value = -TIME_ROOT * (both[:slots] + both[slots:])
        for s in range(own):
            value += jnp.where(rows == s * devices + place[0], noise[s : s + 1, at], 0.0)
        out[:, at] = value
        return carry

    lax.fori_loop(0, count, step, 0)


def partial_fields(own, half, place, rotated, contracted, noise):
    vectors, columns = contracted.shape
    devices = rotated.shape[0]
    count = vectors // 512
    return pl.pallas_call(
        functools.partial(bias_kernel, own, half),
        grid=(1,),
        out_shape=jax.ShapeDtypeStruct((own * devices, vectors), F32),
        in_specs=[
            pl.BlockSpec(memory_space=pltpu.SMEM),
            whole(rotated.shape),
            whole(noise.shape),
            pl.BlockSpec(memory_space=pl.ANY),
        ],
        out_specs=whole((own * devices, vectors)),
        scratch_shapes=[
            pltpu.VMEM((2 * own * devices, columns), BF16),
            pltpu.VMEM(contracted.shape, F32),
            pltpu.SemaphoreType.DMA((count,)),
        ],
        compiler_params=params(52),
    )(place, rotated, noise, contracted)


def send(x, walk_size, chol_size, target):
    return lax.ppermute(x, BOTH, [(i, target(i)) for i in range(walk_size * chol_size)])


def sum_everywhere(x, walk_size, chol_size):
    walk = lax.axis_index("walk")
    core = lax.axis_index("chol") % 2
    half = x.shape[0] // 2
    quarter = half // walk_size
    mine = lax.dynamic_slice_in_dim(x, core * half, half, 0)
    other = lax.dynamic_slice_in_dim(x, (1 - core) * half, half, 0)
    chip = mine + send(other, walk_size, chol_size, lambda i: i ^ 1)
    total = lax.dynamic_slice_in_dim(chip, walk * quarter, quarter, 0)
    got = [
        send(
            lax.dynamic_slice_in_dim(chip, (walk ^ r) * quarter, quarter, 0),
            walk_size, chol_size, lambda i, r=r: i ^ (r * chol_size),
        )
        for r in range(1, walk_size)
    ]
    for g in got:
        total = total + g
    got = [send(total, walk_size, chol_size, lambda i, r=r: i ^ (2 * r)) for r in range(1, chol_size // 2)]
    for g in got:
        total = total + g
    blocks = [total] + [
        send(total, walk_size, chol_size, lambda i, r=r: i ^ (r * chol_size)) for r in range(1, walk_size)
    ]
    here = jnp.concatenate(blocks, axis=0)
    there = send(here, walk_size, chol_size, lambda i: i ^ 1)
    return jnp.concatenate([here, there], axis=0)


def row_of(walker, own, walk_size, chol_size):
    everyone = own * walk_size * chol_size
    walk = lax.axis_index("walk")
    core = lax.axis_index("chol") % 2
    row = (walker % own) * (walk_size * chol_size) + walker // own
    half = everyone // 2
    quarter = half // walk_size
    inside = row % half
    return ((row // half) ^ core) * half + ((inside // quarter) ^ walk) * quarter + inside % quarter


def select(rows, summed, out):
    slots, vectors = summed.shape
    lane = jax.lax.broadcasted_iota(jnp.int32, (slots, slots), 1)
    pick = jnp.where(lane == rows[...], 1.0, 0.0).astype(BF16)
    block = 512
    for g in range(0, vectors, block):
        value = summed[:, g : g + block]
        first, rest = split(value)
        second, third = split(value - first.astype(F32))
        picked = dot(pick, first) + dot(pick, second) + dot(pick, third)
        high, low = split(TIME_ROOT * picked)
        out[:slots, g : g + block] = high
        out[slots:, g : g + block] = low


def carry_kernel(own, half, rows, received, out):
    devices = received.shape[0]
    slots = own * devices
    lane = jax.lax.broadcasted_iota(jnp.int32, (slots, slots), 1)
    pick = jnp.where(lane == rows[...], 1.0, 0.0).astype(BF16)
    for i in range(half):
        value = jnp.concatenate([received[:, (own + s) * half + i, :] for s in range(own)], axis=0)
        first, rest = split(value)
        second, third = split(value - first.astype(F32))
        picked = dot(pick, first) + dot(pick, second) + dot(pick, third)
        for s in range(own):
            out[s * half + i] = picked[s * devices : (s + 1) * devices]


def carry(own, half, rows, received):
    devices = received.shape[0]
    shape = (own * half, devices, LANES)
    return pl.pallas_call(
        functools.partial(carry_kernel, own, half),
        grid=(1,),
        out_shape=jax.ShapeDtypeStruct(shape, F32),
        in_specs=[whole((own * devices, 1)), whole(received.shape)],
        out_specs=whole(shape),
        compiler_params=params(16),
    )(rows.reshape(-1, 1), received)


def potential_kernel(own, parts, base, *refs):
    chols = refs[:parts]
    if len(refs) == parts + 2:
        fields, out = refs[parts:]
    else:
        orbital_rows, summed, noise, rows, places, levels, out, fields = refs[parts:]

        @pl.when(pl.program_id(0) == 0)
        def _():
            select(rows, summed, fields)

    slots = fields.shape[0] // 2
    devices = slots // own
    unit = SUBLANES // own
    step = chols[0].shape[0]
    pieces = chols[0].shape[1] // LANES
    total = None
    for p in range(parts):
        high, low = split(chols[p][...])
        part = fields[:, p * step : (p + 1) * step]
        value = dot(part, high) + dot(part, low)
        total = value if total is None else total + value
    total = total[:slots] + total[slots:]
    here = pl.program_id(0)
    start = here // unit * (pieces * SUBLANES) + here % unit
    stride = out.shape[0] // devices
    for t in range(pieces):
        for s in range(own):
            at = pl.ds(start + t * SUBLANES + s * unit, devices, stride=stride)
            out[at, :] = total[s * devices : (s + 1) * devices, t * LANES : (t + 1) * LANES]
    if len(refs) == parts + 2:
        return

    @pl.when(here == 0)
    def _():
        lane = jax.lax.broadcasted_iota(jnp.int32, (1, LANES), 1)
        line = jnp.zeros((1, LANES), F32)
        for s in range(own):
            shift = noise[s : s + 1, :] - summed[pl.ds(places[s], 1), :]
            terms = 0.5 * shift * shift - noise[s : s + 1, :] * shift
            line = jnp.where(lane == s, levels[s] + jnp.sum(terms, axis=1, keepdims=True), line)
        taken = orbital_rows.shape[0]
        for r in range(taken):
            out[pl.ds(base + r, devices, stride=stride), :] = orbital_rows[r]
        for r in range(taken, stride - base):
            out[pl.ds(base + r, devices, stride=stride), :] = jnp.broadcast_to(line, (devices, LANES))


def potential_tiles(own, fields, chol, orbitals, first, count, along):
    vectors = chol.shape[0]
    slots = along[1].shape[0] if along else fields.shape[0] // 2
    step = 256
    parts = vectors // step
    devices = slots // own
    base = own * count * orbitals // LANES
    rows = devices * base
    smem = pl.BlockSpec(memory_space=pltpu.SMEM)
    more, shapes = along, []
    specs = [whole(fields.shape)] if not along else [whole(a.shape) for a in along[:4]] + [smem, smem]
    if along:
        rows += devices * eights(along[0].shape[0] + 1)
        shapes = [jax.ShapeDtypeStruct((2 * slots, vectors), BF16)]
    else:
        more = (fields,)
    shapes = [jax.ShapeDtypeStruct((rows, LANES), F32)] + shapes
    return pl.pallas_call(
        functools.partial(potential_kernel, own, parts, base),
        grid=(count,),
        out_shape=shapes,
        in_specs=[pl.BlockSpec((step, orbitals), lambda i, p=p: (p, first + i)) for p in range(parts)]
        + specs,
        out_specs=[whole(shape.shape) for shape in shapes],
        compiler_params=params(32),
        cost_estimate=pl.CostEstimate(
            flops=2 * slots * vectors * orbitals * count * 3,
            bytes_accessed=4 * vectors * orbitals * count,
            transcendentals=0,
        ),
    )(*[chol] * parts, *more)


def taylor_kernel(own, chunks, base, *refs):
    tiles = refs[:chunks]
    begin = refs[chunks:-4]
    out, high, low, term = refs[-4:]
    orbitals, width = term.shape
    occupied = width // own
    pieces = orbitals // LANES
    devices = tiles[0].shape[0]
    half = orbitals // devices // 2
    unit = SUBLANES // own
    lane = jax.lax.broadcasted_iota(jnp.int32, (1, width), 1) // occupied
    sub = jax.lax.broadcasted_iota(jnp.int32, (SUBLANES, 1), 0) // unit
    for t in range(pieces):
        parts = []
        for c, tile in enumerate(tiles):
            value = tile[:, :base, :] if c == 0 else tile[...]
            parts.append(value.reshape(devices, -1, pieces, SUBLANES, LANES)[:, :, t])
        value_high, value_low = split(jnp.concatenate(parts, axis=1).reshape(-1, LANES))
        high[:, t * LANES : (t + 1) * LANES] = value_high
        low[:, t * LANES : (t + 1) * LANES] = value_low
    if begin:
        total = begin[0][...]
    else:
        left = tiles[0][:, base : base + half, :]
        right = tiles[0][:, base + half : base + 2 * half, :]
        upper = jnp.where(lane == 0, left, pltpu.roll(right, occupied, 2))
        lower = jnp.where(lane == 0, pltpu.roll(left, occupied, 2), right)
        total = jnp.stack([upper, lower], axis=1).reshape(orbitals, width)
    term[...] = total
    for order in range(1, TERMS):
        term_high, term_low = split(term[...])
        pair = jnp.concatenate([term_high, term_low], axis=1)
        both = dot(high[...], pair)
        value = both[:, :width] + both[:, width:] + dot(low[...], term_high)
        value = value.reshape(-1, own, SUBLANES, width)
        placed = jnp.zeros((value.shape[0], SUBLANES, width), F32)
        for j in range(own):
            for s in range(own):
                shift = ((j - s) * unit) % SUBLANES
                moved = pltpu.roll(value[:, j], shift, 1) if shift else value[:, j]
                placed = jnp.where((sub == j) & (lane == s), moved, placed)
        placed = placed.reshape(orbitals, width) / order
        term[...] = placed
        total = total + placed
    flipped = total.T
    for s in range(own):
        out[s] = flipped[s * occupied : (s + 1) * occupied, :]


def taylor(tiles, base, own, orbitals, occupied):
    width = own * occupied
    chunks = len(tiles)
    devices = tiles[0].shape[0]
    half = orbitals // devices // 2
    begin = []
    if half % SUBLANES or own != 2:
        start = tiles[0][:, base : base + own * half].reshape(devices, own, half, 2, occupied)
        begin = [start.transpose(0, 3, 2, 1, 4).reshape(orbitals, width)]
    vmem = pl.BlockSpec(memory_space=pltpu.VMEM)
    return pl.pallas_call(
        functools.partial(taylor_kernel, own, chunks, base),
        out_shape=jax.ShapeDtypeStruct((own, occupied, orbitals), F32),
        in_specs=[vmem] * (chunks + len(begin)),
        out_specs=vmem,
        scratch_shapes=[
            pltpu.VMEM((own * orbitals, orbitals), BF16),
            pltpu.VMEM((own * orbitals, orbitals), BF16),
            pltpu.VMEM((orbitals, width), F32),
        ],
        compiler_params=params(24),
    )(*tiles, *begin)


def per_device(trial, walkers, chol, field_noise, log_weight, parent):
    own, orbitals, occupied = walkers.shape
    walk_size = lax.axis_size("walk")
    chol_size = lax.axis_size("chol")
    devices = walk_size * chol_size
    vectors, pairs = chol.shape
    rows_here = pairs // orbitals
    half = rows_here // 2
    place = lax.axis_index(BOTH)

    sent, pair, begun = rotate(devices, parent, trial.T, walkers.transpose(0, 2, 1), chol)
    rotated = lax.all_to_all(sent, BOTH, split_axis=0, concat_axis=0, tiled=True)
    contracted = contract(pair, chol, begun)
    mine = partial_fields(own, half, place.reshape(1), rotated, contracted, field_noise)
    fields = sum_everywhere(mine, walk_size, chol_size)

    parents = rotated[:, 2 * own * half, :own].T.reshape(own * devices).astype(jnp.int32)
    orbital_rows = carry(own, half, (parents % own) * devices + parents // own, rotated)
    parent_rows = row_of(parents, own, walk_size, chol_size).reshape(-1, 1)
    scaled = []
    places = row_of(place * own + jnp.arange(own, dtype=jnp.int32), own, walk_size, chol_size)

    unit = SUBLANES // own
    units = rows_here // unit
    cuts = [0] + ([FIRST_UNITS] if units > FIRST_UNITS else []) + [units]
    tiles = []
    for begin, end in zip(cuts[:-1], cuts[1:]):
        along = () if begin else (orbital_rows, fields, field_noise, parent_rows, places, log_weight)
        chunk, *more = potential_tiles(
            own, scaled[0] if begin else None, chol, orbitals, begin * unit, (end - begin) * unit, along
        )
        scaled += more
        chunk = chunk.reshape(devices, -1, LANES)
        tiles.append(lax.all_to_all(chunk, BOTH, split_axis=0, concat_axis=0, tiled=True))

    base = own * cuts[1] * unit * orbitals // LANES
    new_walkers = taylor(tiles, base, own, orbitals, occupied).transpose(0, 2, 1)
    new_log_weight = tiles[0][parent // own, base + own * half, parent % own]
    return (new_walkers, new_log_weight)


def solution(mesh):
    return jax.shard_map(
        per_device,
        mesh=mesh,
        in_specs=(
            P(),
            P(BOTH, None, None),
            P(None, BOTH),
            P(BOTH, None),
            P(BOTH),
            P(BOTH),
        ),
        out_specs=(P(BOTH, None, None), P(BOTH)),
        check_vma=False,
    )
```

```python
import functools

import jax
import jax.numpy as jnp
from jax import lax
from jax.experimental import pallas as pl
from jax.experimental.pallas import tpu as pltpu
from jax.sharding import PartitionSpec as P

TERMS = 6
PRECISE = lax.Precision.HIGHEST
TIME_ROOT = 0.1
BOTH = ("walk", "chol")
LANES = 128
SUBLANES = 8
F32 = jnp.float32
BF16 = jnp.bfloat16
MIB = 1024 * 1024
FIRST_UNITS = 1
HEAD = 1024
PIECE = 128


def params(mib):
    return pltpu.CompilerParams(vmem_limit_bytes=mib * MIB)


def whole(shape):
    zeros = (0,) * len(shape)
    return pl.BlockSpec(shape, lambda *_: zeros)


def dot(a, b):
    return jnp.dot(a, b, preferred_element_type=F32)


def dot_nt(a, b):
    return lax.dot_general(a, b, (((1,), (1,)), ((), ())), preferred_element_type=F32)


def split(x):
    high = x.astype(BF16)
    low = (x - high.astype(F32)).astype(BF16)
    return high, low


def rotate_kernel(devices, parent, trial_in, walkers_in, chol, sent, pair, contracted, trial, walkers, loaded, done, sems):
    own, occupied, orbitals = walkers.shape
    half = orbitals // devices // 2
    count = loaded.shape[0] // PIECE
    small = [
        pltpu.make_async_copy(walkers_in, walkers, sems.at[0]),
        pltpu.make_async_copy(trial_in, trial, sems.at[1]),
    ]
    reads, writes = [], []
    for p in range(count):
        at = pl.ds(p * PIECE, PIECE)
        reads.append(pltpu.make_async_copy(chol.at[at], loaded.at[at], sems.at[2 + p]))
        writes.append(pltpu.make_async_copy(done.at[at], contracted.at[at], sems.at[2 + count + p]))
    for copy in small + reads:
        copy.start()
    for copy in small:
        copy.wait()
    lane = jax.lax.broadcasted_iota(jnp.int32, (1, LANES), 1)
    both_parts = jnp.concatenate([trial[...]] * 2, axis=0).T
    high, low = split(both_parts)
    both_parts = jnp.where(lane < occupied, high, low)
    pair[...] = both_parts
    alone = jnp.where(lane < occupied, both_parts, jnp.zeros_like(both_parts))
    rows = jax.lax.broadcasted_iota(jnp.int32, (occupied, 1), 0)
    state = []
    for s in range(own):
        crossed = lax.dot_general(
            walkers[s], trial[...], (((1,), (1,)), ((), ())), precision=PRECISE, preferred_element_type=F32
        )
        normal = lax.dot_general(
            crossed, crossed, (((1,), (1,)), ((), ())), precision=PRECISE, preferred_element_type=F32
        )
        state.append(jnp.concatenate([normal, crossed], axis=1))

    def eliminate(k):
        for s in range(own):
            m = state[s]
            pivot = m[k : k + 1, :]
            scaled = pivot / m[k : k + 1, k : k + 1]
            state[s] = jnp.where(rows == k, scaled, m - m[:, k : k + 1] * scaled)

    pivots = 0
    for p in range(count):
        reads[p].wait()
        at = slice(p * PIECE, (p + 1) * PIECE)
        for i in range(half):
            ends = [contract_row(loaded[at, r * orbitals : (r + 1) * orbitals], both_parts, alone) for r in (i, i + half)]
            done[at, i * LANES : (i + 1) * LANES] = jnp.where(lane < occupied, ends[0], ends[1])
            upto = occupied * (p * half + i + 1) // (count * half)
            for k in range(pivots, upto):
                eliminate(k)
            pivots = upto
        writes[p].start()
    packed = jnp.concatenate([walkers[s] for s in range(own)], axis=0).T
    empty = jnp.zeros((occupied, occupied), F32)
    inverse = jnp.concatenate(
        [
            jnp.concatenate([state[s][:, occupied:] if s == c else empty for c in range(own)], axis=1)
            for s in range(own)
        ],
        axis=0,
    )
    rotated = jnp.dot(packed, inverse, precision=PRECISE, preferred_element_type=F32)
    for at, value in ((0, rotated), (own * half, packed)):
        blocks = value.reshape(devices, 2, half, LANES)
        first, second = blocks[:, 0], blocks[:, 1]
        sent[:, at : at + half, :] = jnp.where(lane < occupied, first, pltpu.roll(second, occupied, 2))
        sent[:, at + half : at + 2 * half, :] = jnp.where(lane < occupied, pltpu.roll(first, occupied, 2), second)
    extra = jnp.zeros((SUBLANES, LANES), F32)
    for s in range(own):
        extra = jnp.where(lane == s, parent[s].astype(F32), extra)
    tail = sent.shape[1] - 2 * own * half
    sent[:, 2 * own * half :, :] = jnp.broadcast_to(extra[None, :tail], (devices, tail, LANES))
    for copy in writes:
        copy.wait()


def rotate_plain(devices, parent, trial, walkers, sent_rows):
    own, occupied, orbitals = walkers.shape
    half = orbitals // devices // 2
    crossed = jnp.einsum("wkm,nm->wkn", walkers, trial, precision=PRECISE)
    normal = jnp.einsum("wkn,wln->wkl", crossed, crossed, precision=PRECISE)
    factor = jnp.linalg.cholesky(normal)
    inverse = jax.vmap(lambda f, c: jax.scipy.linalg.cho_solve((f, True), c))(factor, crossed)
    rotated = jnp.einsum("wkm,wkn->wmn", walkers, inverse, precision=PRECISE)
    sent = jnp.concatenate([rotated, walkers.transpose(0, 2, 1)], axis=0)
    sent = sent.reshape(2 * own, devices, 2, half, occupied).transpose(1, 0, 3, 2, 4)
    sent = sent.reshape(devices, 2 * own * half, 2 * occupied)
    extra = jnp.zeros((sent_rows - 2 * own * half, LANES), F32).at[0, :own].set(parent.astype(F32))
    sent = jnp.concatenate([sent, jnp.broadcast_to(extra[None], (devices,) + extra.shape)], axis=1)
    return sent, jnp.concatenate(split(trial.T), axis=1)


def eights(rows):
    return -(-rows // SUBLANES) * SUBLANES


def rotate(devices, parent, trial, walkers, chol):
    own, occupied, orbitals = walkers.shape
    vectors = chol.shape[0]
    columns = chol.shape[1] // orbitals * occupied
    half = orbitals // devices // 2
    sent_rows = eights(2 * own * half + 1)
    if half % SUBLANES or own != 2 or own * occupied != LANES:
        return rotate_plain(devices, parent, trial, walkers, sent_rows) + (None,)
    anywhere = pl.BlockSpec(memory_space=pl.ANY)
    return pl.pallas_call(
        functools.partial(rotate_kernel, devices),
        grid=(1,),
        out_shape=(
            jax.ShapeDtypeStruct((devices, sent_rows, LANES), F32),
            jax.ShapeDtypeStruct((orbitals, 2 * occupied), BF16),
            jax.ShapeDtypeStruct((vectors, columns), F32),
        ),
        in_specs=[pl.BlockSpec(memory_space=pltpu.SMEM), anywhere, anywhere, anywhere],
        out_specs=(whole((devices, sent_rows, LANES)), whole((orbitals, 2 * occupied)), anywhere),
        scratch_shapes=[
            pltpu.VMEM(trial.shape, F32),
            pltpu.VMEM(walkers.shape, F32),
            pltpu.VMEM((HEAD, chol.shape[1]), F32),
            pltpu.VMEM((HEAD, columns), F32),
            pltpu.SemaphoreType.DMA((2 + 2 * (HEAD // PIECE),)),
        ],
        compiler_params=params(60),
    )(parent, trial, walkers, chol)


def contract_row(part, both_parts, alone):
    chol_high, chol_low = split(part)
    both = dot(chol_high, both_parts) + dot(chol_low, alone)
    return both + pltpu.roll(both, both.shape[1] // 2, 1)


def contract_kernel(pair, chol, *refs):
    out = refs[-1]
    orbitals = pair.shape[0]
    occupied = pair.shape[1] // 2
    half = chol.shape[1] // orbitals // 2
    lane = jax.lax.broadcasted_iota(jnp.int32, (1, 2 * occupied), 1)
    both_parts = pair[...]
    alone = jnp.where(lane < occupied, both_parts, jnp.zeros_like(both_parts))
    for i in range(half):
        ends = [contract_row(chol[:, r * orbitals : (r + 1) * orbitals], both_parts, alone) for r in (i, i + half)]
        out[:, i * 2 * occupied : (i + 1) * 2 * occupied] = jnp.where(lane < occupied, ends[0], ends[1])


def contract(pair, chol, begun):
    vectors, pairs = chol.shape
    orbitals, occupied = pair.shape[0], pair.shape[1] // 2
    columns = pairs // orbitals * occupied
    block = 256
    skip = 0 if begun is None else HEAD // block
    more = [] if begun is None else [begun]
    rest = vectors - skip * block
    return pl.pallas_call(
        contract_kernel,
        grid=(rest // block,),
        out_shape=jax.ShapeDtypeStruct((vectors, columns), F32),
        in_specs=[whole(pair.shape), pl.BlockSpec((block, pairs), lambda g: (g + skip, 0))]
        + [pl.BlockSpec(memory_space=pl.ANY)] * len(more),
        out_specs=pl.BlockSpec((block, columns), lambda g: (g + skip, 0)),
        input_output_aliases={2: 0} if more else {},
        compiler_params=params(60),
        cost_estimate=pl.CostEstimate(
            flops=2 * rest * pairs * occupied * 3, bytes_accessed=4 * rest * (pairs + columns), transcendentals=0
        ),
    )(pair, chol, *more)


def bias_kernel(own, half, place, rotated, noise, contracted, out, stacked, loaded, sems):
    devices = rotated.shape[0]
    slots = own * devices
    count = sems.shape[0]
    block = loaded.shape[0] // count
    copies = []
    for g in range(count):
        at = pl.ds(g * block, block)
        copies.append(pltpu.make_async_copy(contracted.at[at], loaded.at[at], sems.at[g]))
    for copy in copies:
        copy.start()
    for i in range(half):
        for s in range(own):
            high, low = split(rotated[:, s * half + i, :])
            at = s * devices
            stacked[at : at + devices, i * LANES : (i + 1) * LANES] = high
            stacked[slots + at : slots + at + devices, i * LANES : (i + 1) * LANES] = low
    rows = jax.lax.broadcasted_iota(jnp.int32, (slots, 1), 0)

    def step(g, carry):
        at = pl.ds(pl.multiple_of(g * block, LANES), block)
        pltpu.make_async_copy(contracted.at[at], loaded.at[at], sems.at[g]).wait()
        b_high, b_low = split(loaded[at, :])
        both = dot_nt(stacked[...], b_high) + dot_nt(stacked[...], b_low)
        value = -TIME_ROOT * (both[:slots] + both[slots:])
        for s in range(own):
            value += jnp.where(rows == s * devices + place[0], noise[s : s + 1, at], 0.0)
        out[:, at] = value
        return carry

    lax.fori_loop(0, count, step, 0)


def partial_fields(own, half, place, rotated, contracted, noise):
    vectors, columns = contracted.shape
    devices = rotated.shape[0]
    count = vectors // 512
    return pl.pallas_call(
        functools.partial(bias_kernel, own, half),
        grid=(1,),
        out_shape=jax.ShapeDtypeStruct((own * devices, vectors), F32),
        in_specs=[
            pl.BlockSpec(memory_space=pltpu.SMEM),
            whole(rotated.shape),
            whole(noise.shape),
            pl.BlockSpec(memory_space=pl.ANY),
        ],
        out_specs=whole((own * devices, vectors)),
        scratch_shapes=[
            pltpu.VMEM((2 * own * devices, columns), BF16),
            pltpu.VMEM(contracted.shape, F32),
            pltpu.SemaphoreType.DMA((count,)),
        ],
        compiler_params=params(52),
    )(place, rotated, noise, contracted)


def send(x, walk_size, chol_size, target):
    return lax.ppermute(x, BOTH, [(i, target(i)) for i in range(walk_size * chol_size)])


def sum_everywhere(x, walk_size, chol_size):
    walk = lax.axis_index("walk")
    core = lax.axis_index("chol") % 2
    half = x.shape[0] // 2
    quarter = half // walk_size
    mine = lax.dynamic_slice_in_dim(x, core * half, half, 0)
    other = lax.dynamic_slice_in_dim(x, (1 - core) * half, half, 0)
    chip = mine + send(other, walk_size, chol_size, lambda i: i ^ 1)
    total = lax.dynamic_slice_in_dim(chip, walk * quarter, quarter, 0)
    got = [
        send(
            lax.dynamic_slice_in_dim(chip, (walk ^ r) * quarter, quarter, 0),
            walk_size, chol_size, lambda i, r=r: i ^ (r * chol_size),
        )
        for r in range(1, walk_size)
    ]
    for g in got:
        total = total + g
    got = [send(total, walk_size, chol_size, lambda i, r=r: i ^ (2 * r)) for r in range(1, chol_size // 2)]
    for g in got:
        total = total + g
    blocks = [total] + [
        send(total, walk_size, chol_size, lambda i, r=r: i ^ (r * chol_size)) for r in range(1, walk_size)
    ]
    here = jnp.concatenate(blocks, axis=0)
    there = send(here, walk_size, chol_size, lambda i: i ^ 1)
    return jnp.concatenate([here, there], axis=0)


def row_of(walker, own, walk_size, chol_size):
    everyone = own * walk_size * chol_size
    walk = lax.axis_index("walk")
    core = lax.axis_index("chol") % 2
    row = (walker % own) * (walk_size * chol_size) + walker // own
    half = everyone // 2
    quarter = half // walk_size
    inside = row % half
    return ((row // half) ^ core) * half + ((inside // quarter) ^ walk) * quarter + inside % quarter


def select(rows, summed, out):
    slots, vectors = summed.shape
    lane = jax.lax.broadcasted_iota(jnp.int32, (slots, slots), 1)
    pick = jnp.where(lane == rows[...], 1.0, 0.0).astype(BF16)
    block = 512
    for g in range(0, vectors, block):
        value = summed[:, g : g + block]
        first, rest = split(value)
        second, third = split(value - first.astype(F32))
        picked = dot(pick, first) + dot(pick, second) + dot(pick, third)
        high, low = split(TIME_ROOT * picked)
        out[:slots, g : g + block] = high
        out[slots:, g : g + block] = low


def carry_kernel(own, half, rows, received, out):
    devices = received.shape[0]
    slots = own * devices
    lane = jax.lax.broadcasted_iota(jnp.int32, (slots, slots), 1)
    pick = jnp.where(lane == rows[...], 1.0, 0.0).astype(BF16)
    for i in range(half):
        value = jnp.concatenate([received[:, (own + s) * half + i, :] for s in range(own)], axis=0)
        first, rest = split(value)
        second, third = split(value - first.astype(F32))
        picked = dot(pick, first) + dot(pick, second) + dot(pick, third)
        for s in range(own):
            out[s * half + i] = picked[s * devices : (s + 1) * devices]


def carry(own, half, rows, received):
    devices = received.shape[0]
    shape = (own * half, devices, LANES)
    return pl.pallas_call(
        functools.partial(carry_kernel, own, half),
        grid=(1,),
        out_shape=jax.ShapeDtypeStruct(shape, F32),
        in_specs=[whole((own * devices, 1)), whole(received.shape)],
        out_specs=whole(shape),
        compiler_params=params(16),
    )(rows.reshape(-1, 1), received)


def potential_kernel(own, parts, base, *refs):
    chols = refs[:parts]
    if len(refs) == parts + 2:
        fields, out = refs[parts:]
    else:
        orbital_rows, summed, noise, rows, places, levels, out, fields = refs[parts:]

        @pl.when(pl.program_id(0) == 0)
        def _():
            select(rows, summed, fields)

    slots = fields.shape[0] // 2
    devices = slots // own
    unit = SUBLANES // own
    step = chols[0].shape[0]
    pieces = chols[0].shape[1] // LANES
    total = None
    for p in range(parts):
        high, low = split(chols[p][...])
        part = fields[:, p * step : (p + 1) * step]
        value = dot(part, high) + dot(part, low)
        total = value if total is None else total + value
    total = total[:slots] + total[slots:]
    here = pl.program_id(0)
    start = here // unit * (pieces * SUBLANES) + here % unit
    stride = out.shape[0] // devices
    for t in range(pieces):
        for s in range(own):
            at = pl.ds(start + t * SUBLANES + s * unit, devices, stride=stride)
            out[at, :] = total[s * devices : (s + 1) * devices, t * LANES : (t + 1) * LANES]
    if len(refs) == parts + 2:
        return

    @pl.when(here == 0)
    def _():
        lane = jax.lax.broadcasted_iota(jnp.int32, (1, LANES), 1)
        line = jnp.zeros((1, LANES), F32)
        for s in range(own):
            shift = noise[s : s + 1, :] - summed[pl.ds(places[s], 1), :]
            terms = 0.5 * shift * shift - noise[s : s + 1, :] * shift
            line = jnp.where(lane == s, levels[s] + jnp.sum(terms, axis=1, keepdims=True), line)
        taken = orbital_rows.shape[0]
        for r in range(taken):
            out[pl.ds(base + r, devices, stride=stride), :] = orbital_rows[r]
        for r in range(taken, stride - base):
            out[pl.ds(base + r, devices, stride=stride), :] = jnp.broadcast_to(line, (devices, LANES))


def potential_tiles(own, fields, chol, orbitals, first, count, along):
    vectors = chol.shape[0]
    slots = along[1].shape[0] if along else fields.shape[0] // 2
    step = 256
    parts = vectors // step
    devices = slots // own
    base = own * count * orbitals // LANES
    rows = devices * base
    smem = pl.BlockSpec(memory_space=pltpu.SMEM)
    more, shapes = along, []
    specs = [whole(fields.shape)] if not along else [whole(a.shape) for a in along[:4]] + [smem, smem]
    if along:
        rows += devices * eights(along[0].shape[0] + 1)
        shapes = [jax.ShapeDtypeStruct((2 * slots, vectors), BF16)]
    else:
        more = (fields,)
    shapes = [jax.ShapeDtypeStruct((rows, LANES), F32)] + shapes
    return pl.pallas_call(
        functools.partial(potential_kernel, own, parts, base),
        grid=(count,),
        out_shape=shapes,
        in_specs=[pl.BlockSpec((step, orbitals), lambda i, p=p: (p, first + i)) for p in range(parts)]
        + specs,
        out_specs=[whole(shape.shape) for shape in shapes],
        compiler_params=params(32),
        cost_estimate=pl.CostEstimate(
            flops=2 * slots * vectors * orbitals * count * 3,
            bytes_accessed=4 * vectors * orbitals * count,
            transcendentals=0,
        ),
    )(*[chol] * parts, *more)


def taylor_kernel(own, chunks, base, *refs):
    tiles = refs[:chunks]
    begin = refs[chunks:-4]
    out, high, low, term = refs[-4:]
    orbitals, width = term.shape
    occupied = width // own
    pieces = orbitals // LANES
    devices = tiles[0].shape[0]
    half = orbitals // devices // 2
    unit = SUBLANES // own
    lane = jax.lax.broadcasted_iota(jnp.int32, (1, width), 1) // occupied
    sub = jax.lax.broadcasted_iota(jnp.int32, (SUBLANES, 1), 0) // unit
    for t in range(pieces):
        parts = []
        for c, tile in enumerate(tiles):
            value = tile[:, :base, :] if c == 0 else tile[...]
            parts.append(value.reshape(devices, -1, pieces, SUBLANES, LANES)[:, :, t])
        value_high, value_low = split(jnp.concatenate(parts, axis=1).reshape(-1, LANES))
        high[:, t * LANES : (t + 1) * LANES] = value_high
        low[:, t * LANES : (t + 1) * LANES] = value_low
    if begin:
        total = begin[0][...]
    else:
        left = tiles[0][:, base : base + half, :]
        right = tiles[0][:, base + half : base + 2 * half, :]
        upper = jnp.where(lane == 0, left, pltpu.roll(right, occupied, 2))
        lower = jnp.where(lane == 0, pltpu.roll(left, occupied, 2), right)
        total = jnp.stack([upper, lower], axis=1).reshape(orbitals, width)
    term[...] = total
    for order in range(1, TERMS):
        term_high, term_low = split(term[...])
        pair = jnp.concatenate([term_high, term_low], axis=1)
        both = dot(high[...], pair)
        value = both[:, :width] + both[:, width:] + dot(low[...], term_high)
        value = value.reshape(-1, own, SUBLANES, width)
        placed = jnp.zeros((value.shape[0], SUBLANES, width), F32)
        for j in range(own):
            for s in range(own):
                shift = ((j - s) * unit) % SUBLANES
                moved = pltpu.roll(value[:, j], shift, 1) if shift else value[:, j]
                placed = jnp.where((sub == j) & (lane == s), moved, placed)
        placed = placed.reshape(orbitals, width) / order
        term[...] = placed
        total = total + placed
    flipped = total.T
    for s in range(own):
        out[s] = flipped[s * occupied : (s + 1) * occupied, :]


def taylor(tiles, base, own, orbitals, occupied):
    width = own * occupied
    chunks = len(tiles)
    devices = tiles[0].shape[0]
    half = orbitals // devices // 2
    begin = []
    if half % SUBLANES or own != 2:
        start = tiles[0][:, base : base + own * half].reshape(devices, own, half, 2, occupied)
        begin = [start.transpose(0, 3, 2, 1, 4).reshape(orbitals, width)]
    vmem = pl.BlockSpec(memory_space=pltpu.VMEM)
    return pl.pallas_call(
        functools.partial(taylor_kernel, own, chunks, base),
        out_shape=jax.ShapeDtypeStruct((own, occupied, orbitals), F32),
        in_specs=[vmem] * (chunks + len(begin)),
        out_specs=vmem,
        scratch_shapes=[
            pltpu.VMEM((own * orbitals, orbitals), BF16),
            pltpu.VMEM((own * orbitals, orbitals), BF16),
            pltpu.VMEM((orbitals, width), F32),
        ],
        compiler_params=params(24),
    )(*tiles, *begin)


def per_device(trial, walkers, chol, field_noise, log_weight, parent):
    own, orbitals, occupied = walkers.shape
    walk_size = lax.axis_size("walk")
    chol_size = lax.axis_size("chol")
    devices = walk_size * chol_size
    vectors, pairs = chol.shape
    rows_here = pairs // orbitals
    half = rows_here // 2
    place = lax.axis_index(BOTH)

    sent, pair, begun = rotate(devices, parent, trial.T, walkers.transpose(0, 2, 1), chol)
    rotated = lax.all_to_all(sent, BOTH, split_axis=0, concat_axis=0, tiled=True)
    contracted = contract(pair, chol, begun)
    mine = partial_fields(own, half, place.reshape(1), rotated, contracted, field_noise)
    fields = sum_everywhere(mine, walk_size, chol_size)

    parents = rotated[:, 2 * own * half, :own].T.reshape(own * devices).astype(jnp.int32)
    orbital_rows = carry(own, half, (parents % own) * devices + parents // own, rotated)
    parent_rows = row_of(parents, own, walk_size, chol_size).reshape(-1, 1)
    scaled = []
    places = row_of(place * own + jnp.arange(own, dtype=jnp.int32), own, walk_size, chol_size)

    unit = SUBLANES // own
    units = rows_here // unit
    cuts = [0] + ([FIRST_UNITS] if units > FIRST_UNITS else []) + [units]
    tiles = []
    for begin, end in zip(cuts[:-1], cuts[1:]):
        along = () if begin else (orbital_rows, fields, field_noise, parent_rows, places, log_weight)
        chunk, *more = potential_tiles(
            own, scaled[0] if begin else None, chol, orbitals, begin * unit, (end - begin) * unit, along
        )
        scaled += more
        chunk = chunk.reshape(devices, -1, LANES)
        tiles.append(lax.all_to_all(chunk, BOTH, split_axis=0, concat_axis=0, tiled=True))

    base = own * cuts[1] * unit * orbitals // LANES
    new_walkers = taylor(tiles, base, own, orbitals, occupied).transpose(0, 2, 1)
    new_log_weight = tiles[0][parent // own, base + own * half, parent % own]
    return (new_walkers, new_log_weight)


def solution(mesh):
    return jax.shard_map(
        per_device,
        mesh=mesh,
        in_specs=(
            P(),
            P(BOTH, None, None),
            P(None, BOTH),
            P(BOTH, None),
            P(BOTH),
            P(BOTH),
        ),
        out_specs=(P(BOTH, None, None), P(BOTH)),
        check_vma=False,
    )
```
